128 devices in a mesh: dp: 8 (over z, core), context: 4 (over y), tensor: 4 (over x).
Axes of the slice: x: 4, y: 4, z: 4, core: 2. Of those that a mesh axis runs over, the one named last changes fastest.
Arguments:
- hidden: bfloat16 [8, 1024, 8192], P('dp', 'context'), may hold values from -6 to 6
- inputs: bfloat16 [8, 1024, 8192], P('dp', 'context', 'tensor'), may hold values from -6 to 6
- upstream: bfloat16 [8, 1024, 8192], P('dp', 'context', 'tensor'), may hold values from -0.059814453 to 0.059814453
- proj_weight: bfloat16 [2048, 8192], P('tensor', ('dp', 'context')), may hold values from -0.0625 to 0.0625
- delta_weight: bfloat16 [128, 8192], P('tensor', ('dp', 'context')), may hold values from -0.0625 to 0.0625
- decay_rate: float32 [128], P('tensor'), may hold values from 9.765625e-05 to 0.125
- step_bias: float32 [128], P('tensor'), may hold values from -3 to 0
- proj_moment: float32 [2048, 8192], P('tensor', ('dp', 'context')), may hold values from -0.2 to 0.2
- proj_second: float32 [2048, 8192], P('tensor', ('dp', 'context')), may hold values from 0.0001 to 0.01
- delta_moment: float32 [128, 8192], P('tensor', ('dp', 'context')), may hold values from -0.2 to 0.2
- delta_second: float32 [128, 8192], P('tensor', ('dp', 'context')), may hold values from 0.0001 to 0.01
- doc_lengths: int32 [8, 4], P('dp'), may hold values from 1 to 512, 1024 in all within a row
- valid_counts: int32 [8, 4], P('dp', 'context'), may hold values from 64 to 256, as said below
Outputs:
- input_grad: bfloat16 [8, 1024, 8192], P('dp', 'context', 'tensor')
- hidden_grad: bfloat16 [8, 1024, 8192], P('dp', 'context', 'tensor')
- rate_grad: float32 [128], P('tensor')
- bias_grad: float32 [128], P('tensor')
- proj_update: float32 [2048, 8192], P('tensor', ('dp', 'context'))
- delta_update: float32 [128, 8192], P('tensor', ('dp', 'context'))
The draws below stay inside these ranges and needn't reach their ends.
Inputs may be any that keep to these rules, and one draw needn't show every extreme that they name: `doc_lengths`: the 4 lengths of a row sum to 1024, and the longest is exactly half of 1024. The first valid_counts[b, j] tokens of block j of row b are real, the rest padding; in every draw some block is full and another holds exactly 64.
All inputs are finite; a program needn't handle non-finite values.
Results may differ from the reference program's by a relative error of at most 0.014.
Values may be sent and summed in bfloat16 or wider, within the bound.
A program may use at most 128 MiB of HBM per device.

```python
import math
import jax
import jax.numpy as jnp
import numpy as np
from jax import lax

D = 8192
H = 128
HEAD_DIM = 64
N = 256
G = 4
Q = 128
NDOC = 4
TOK_DEV = 256
SEQ = 1024
BATCH = 8
BLOCKS = 4
N_TENSOR = 4


def draw_valid_counts(key, part):
    first = jax.random.fold_in(key, 11)
    second = jax.random.fold_in(key, 23)
    counts = jax.random.randint(first, (BATCH * BLOCKS,), TOK_DEV // 4, TOK_DEV + 1, dtype=jnp.int32)
    spot = jax.random.randint(second, (), 0, BATCH * BLOCKS, dtype=jnp.int32)
    places = jnp.arange(BATCH * BLOCKS, dtype=jnp.int32)
    counts = jnp.where(places == spot, TOK_DEV, counts)
    counts = jnp.where(places == (spot + 1) % (BATCH * BLOCKS), TOK_DEV // 4, counts)
    return counts.reshape(BATCH, BLOCKS).astype(jnp.int32)


def block_levels(stream_key, shape, split, smallest, top_value):
    gain = 1.0
    for position, parts in split:
        heights = jax.random.uniform(jax.random.fold_in(jax.random.fold_in(stream_key, 6), position), (parts,), jnp.float32, smallest / len(split), top_value / len(split))
        gain = gain * jnp.repeat(jnp.exp(heights), shape[position] // parts).reshape((-1,) + (1,) * (len(shape) - 1 - position))
    return gain


def length_profile(count, total, bound, skew):
    weights = [(1 << 20) // math.isqrt(standing ** skew) + 1 for standing in range(2, count + 1)]
    rest, given = total - bound - (count - 1), [1] * (count - 1)
    while rest > 0:
        movable = [i for i in range(count - 1) if given[i] < bound]
        pool, budget = sum([weights[i] for i in movable]), rest
        for i in movable:
            addition = min(bound - given[i], max(1, budget * weights[i] // pool), rest)
            given[i] = given[i] + addition
            rest = rest - addition
    return np.array([bound] + given)


def ragged(stream_key, count, total, most, lean):
    if count == 2:
        one = jax.random.randint(stream_key, (), max(1, total - most), min(most, total - 1) + 1)
        return jnp.stack([one, total - one])
    sizes = jnp.asarray(length_profile(count, total, most, lean), jnp.int32)
    couples = (count - 1) // 2
    source_of, receiver = sizes[1:1 + 2 * couples:2], sizes[2:2 + 2 * couples:2]
    room = jnp.minimum(source_of - 1, most - receiver)
    shifted = jax.random.randint(jax.random.fold_in(stream_key, 1), (couples,), 0, 1 << 20) % (room + 1)
    sizes = sizes.at[1:1 + 2 * couples:2].set(source_of - shifted).at[2:2 + 2 * couples:2].set(receiver + shifted)
    return sizes[jax.random.permutation(jax.random.fold_in(stream_key, 2), count)]


def normal_values(stream_key, shape, scale, most, cuts=(), kind=jnp.bfloat16):
    loudness = block_levels(stream_key, shape, cuts, -0.22, 0.18) if cuts else 1.0
    values = jax.random.normal(stream_key, shape, jnp.float32) * scale * loudness
    return jnp.minimum(jnp.maximum(values, -most), most).astype(kind)


def setup_inputs(seed: int = 0) -> dict:
    keys = jax.random.split(jax.random.key(seed), 14)
    return {
        "hidden": normal_values(keys[0], (BATCH, SEQ, D), 1.0, 6.0, ((0, 8), (1, 4))),
        "inputs": normal_values(keys[1], (BATCH, SEQ, H * HEAD_DIM), 1.0, 6.0, ((0, 8), (1, 4), (2, 4))),
        "upstream": normal_values(keys[2], (BATCH, SEQ, H * HEAD_DIM), 0.01, 0.059814453, ((0, 8), (1, 4), (2, 4))),
        "proj_weight": normal_values(keys[3], (2 * G * N, D), D ** -0.5, 0.0625, ((0, 4), (1, 32))),
        "delta_weight": normal_values(keys[4], (H, D), D ** -0.5, 0.0625, ((0, 4), (1, 32))),
        "decay_rate": jnp.clip(jnp.exp(math.log(0.125) - 7.1546153 * jax.random.uniform(keys[5], (H,), jnp.float32) ** block_levels(keys[5], (H,), ((0, 4),), -0.2, 0.2)), 9.765625145519152e-05, 0.125),
        "step_bias": jnp.clip(-3.0 + 3.0 * jax.random.uniform(keys[6], (H,), jnp.float32) ** block_levels(keys[6], (H,), ((0, 4),), -0.2, 0.2), -3.0, 0.0),
        "proj_moment": normal_values(keys[7], (2 * G * N, D), 0.03, 0.2, ((0, 4), (1, 32)), jnp.float32),
        "proj_second": jnp.clip(jnp.exp(math.log(0.01) - 4.6051702 * jax.random.uniform(keys[8], (2 * G * N, D), jnp.float32) ** block_levels(keys[8], (2 * G * N, D), ((0, 4), (1, 32)), -0.2, 0.2)), 0.0001, 0.01),
        "delta_moment": normal_values(keys[9], (H, D), 0.03, 0.2, ((0, 4), (1, 32)), jnp.float32),
        "delta_second": jnp.clip(jnp.exp(math.log(0.01) - 4.6051702 * jax.random.uniform(keys[10], (H, D), jnp.float32) ** block_levels(keys[10], (H, D), ((0, 4), (1, 32)), -0.2, 0.2)), 0.0001, 0.01),
        "doc_lengths": jax.vmap(lambda own: ragged(own, NDOC, SEQ, SEQ // 2, 2))(jax.random.split(keys[11], BATCH)).reshape((BATCH, NDOC)).astype(jnp.int32),
        "valid_counts": draw_valid_counts(jax.random.fold_in(keys[13], 71), 0),
    }


beta_one = 0.9
beta_two = 0.95
adam_eps = 1e-08
adam_step = 100
highest = lax.Precision.HIGHEST

def prepare(inputs, delta, writes, reads, decay_rate, start):
    tokens, heads, width = inputs.shape
    groups = writes.shape[1]
    per_group = heads // groups
    blocks = tokens // Q
    values = inputs.reshape(blocks, Q, groups, per_group, width)
    steps = jnp.transpose(delta.reshape(blocks, Q, groups, per_group), (0, 2, 3, 1))
    write_blocks = writes.reshape(blocks, Q, groups, -1)
    read_blocks = reads.reshape(blocks, Q, groups, -1)
    logs = jnp.cumsum(-decay_rate.reshape(1, groups, per_group, 1) * steps, axis=3)
    marks = jnp.cumsum(start.reshape(blocks, Q), axis=1)
    return (values, steps, write_blocks, read_blocks, logs, marks)

def state_terms(values, steps, write_blocks, logs, marks):
    same_doc = (marks[:, -1:] == marks)[:, None, None, :]
    tail = jnp.where(same_doc, jnp.exp(logs[..., -1:] - logs), 0.0)
    block_states = jnp.einsum('cgjs,csgjp,csgn->cgjpn', tail * steps, values, write_blocks, precision=highest)
    keeps = jnp.where((marks[:, -1] == 0)[:, None, None], jnp.exp(logs[..., -1]), 0.0)
    return (keeps, block_states)

def ssd_forward(inputs, delta, writes, reads, decay_rate, start, state):
    tokens, heads, width = inputs.shape
    values, steps, write_blocks, read_blocks, logs, marks = prepare(inputs, delta, writes, reads, decay_rate, start)
    order = jnp.arange(Q, dtype=jnp.int32)
    inside = (order[:, None] >= order[None, :])[None] & (marks[:, :, None] == marks[:, None, :])
    inside = inside[:, None, None]
    gaps = jnp.where(inside, logs[..., :, None] - logs[..., None, :], 0.0)
    weights = jnp.where(inside, jnp.exp(gaps), 0.0)
    scores = jnp.einsum('ctgn,csgn->cgts', read_blocks, write_blocks, precision=highest)
    mixing = scores[:, :, None] * weights * steps[:, :, :, None, :]
    local_out = jnp.einsum('cgjts,csgjp->ctgjp', mixing, values, precision=highest)
    keeps, block_states = state_terms(values, steps, write_blocks, logs, marks)

    def advance(carry, pair):
        keep, block_state = pair
        return (keep[..., None, None] * carry + block_state, carry)
    final, entering = lax.scan(advance, state, (keeps, block_states))
    head = jnp.where((marks == 0)[:, None, None, :], jnp.exp(logs), 0.0)
    carried_out = jnp.einsum('cgjt,cgjpn,ctgn->ctgjp', head, entering, read_blocks, precision=highest)
    total = local_out + carried_out
    return (total.reshape(tokens, heads, width), final)

def adam_direction(grad, moment, second):
    moment = beta_one * moment + (1.0 - beta_one) * grad
    second = beta_two * second + (1.0 - beta_two) * grad * grad
    corrected = moment / (1.0 - beta_one ** adam_step)
    return corrected / (jnp.sqrt(second / (1.0 - beta_two ** adam_step)) + adam_eps)

def reference(hidden, inputs, upstream, proj_weight, delta_weight, decay_rate, step_bias, proj_moment, proj_second, delta_moment, delta_second, doc_lengths, valid_counts):
    zero_state = jnp.zeros((G, H // G, HEAD_DIM, N), jnp.float32)

    def one_row(carry, row_data):
        rows, row_inputs, row_upstream, lengths, counts = row_data
        projected = jnp.dot(rows, proj_weight.T, preferred_element_type=jnp.float32)
        projected = lax.optimization_barrier(projected.astype(jnp.bfloat16)).astype(jnp.float32)
        mixed = projected.reshape(SEQ, G, 2, N)
        writes = mixed[:, :, 0]
        reads = mixed[:, :, 1]
        raw = jnp.dot(rows, delta_weight.T, preferred_element_type=jnp.float32) + step_bias
        place = jnp.arange(SEQ, dtype=jnp.int32)
        limit = counts[place // TOK_DEV]
        valid = jnp.where(place % TOK_DEV < limit, 1.0, 0.0).astype(jnp.float32)
        starts = (jnp.cumsum(lengths) - lengths).astype(jnp.int32)
        start = jnp.where(jnp.any(place[:, None] == starts[None, :], axis=1), 1.0, 0.0).astype(jnp.float32)
        delta = valid[:, None] * jax.nn.softplus(raw)
        values = row_inputs.astype(jnp.float32).reshape(SEQ, H, HEAD_DIM)
        grads_in = row_upstream.astype(jnp.float32).reshape(SEQ, H, HEAD_DIM) * valid[:, None, None]

        def local(inputs_here, delta_here, writes_here, reads_here, rate_here):
            return ssd_forward(inputs_here, delta_here, writes_here, reads_here, rate_here, start, zero_state)
        unused, pull = jax.vjp(local, values, delta, writes, reads, decay_rate)
        value_grad, delta_grad, write_grad, read_grad, rate_grad = pull((grads_in, zero_state))
        raw_grad = delta_grad * valid[:, None] * jax.nn.sigmoid(raw)
        write_read = jnp.stack([write_grad, read_grad], axis=2).reshape(SEQ, 2 * G * N).astype(jnp.bfloat16)
        raw_round = raw_grad.astype(jnp.bfloat16)
        pieces = write_read.reshape(SEQ, N_TENSOR, -1).astype(jnp.float32)
        weight_pieces = proj_weight.reshape(N_TENSOR, -1, D).astype(jnp.float32)
        raw_pieces = raw_round.reshape(SEQ, N_TENSOR, -1).astype(jnp.float32)
        delta_pieces = delta_weight.reshape(N_TENSOR, -1, D).astype(jnp.float32)
        partial_value = jnp.einsum('tka,kad->ktd', pieces, weight_pieces, precision=highest)
        partial_value = partial_value + jnp.einsum('tka,kad->ktd', raw_pieces, delta_pieces, precision=highest)
        partial_value = lax.optimization_barrier(partial_value.astype(jnp.bfloat16)).astype(jnp.float32)
        hidden_row = lax.optimization_barrier(jnp.sum(partial_value, axis=0)).astype(jnp.bfloat16)
        proj_acc = carry[0] + jnp.dot(write_read.T, rows, preferred_element_type=jnp.float32)
        delta_acc = carry[1] + jnp.dot(raw_round.T, rows, preferred_element_type=jnp.float32)
        head_acc = carry[2] + jnp.stack([rate_grad, lax.optimization_barrier(jnp.sum(raw_grad, axis=0))])
        input_row = value_grad.reshape(SEQ, H * HEAD_DIM).astype(jnp.bfloat16)
        return ((proj_acc, delta_acc, head_acc), (input_row, hidden_row))
    start_carry = (jnp.zeros((2 * G * N, D), jnp.float32), jnp.zeros((H, D), jnp.float32), jnp.zeros((2, H), jnp.float32))
    sums, outputs = lax.scan(one_row, start_carry, (hidden, inputs, upstream, doc_lengths, valid_counts))
    count = jnp.sum(valid_counts).astype(jnp.float32)
    proj_update = adam_direction(sums[0] / count, proj_moment, proj_second)
    delta_update = adam_direction(sums[1] / count, delta_moment, delta_second)
    return (outputs[0], outputs[1], sums[2][0] / count, sums[2][1] / count, proj_update, delta_update)
```

```python
import functools

import jax
import jax.numpy as jnp
from jax import lax
from jax.experimental import pallas as pl
from jax.experimental.pallas import tpu as pltpu
from jax.sharding import PartitionSpec as P

HEAD_DIM = 64
N = 256
Q = 128
D = 8192
TOK = 256
ROWS = 544
CUT = 272
MESH = pl.DeviceIdType.MESH
f32 = jnp.float32
bf16 = jnp.bfloat16

beta_one = 0.9
beta_two = 0.95
adam_eps = 1e-08
adam_step = 100
highest = lax.Precision.HIGHEST

RING = (0, 1, 2, 1)
PIECES = [(i, j) for i in range(4) for j in range(4)]


def distance(piece):
    return RING[piece[0]] + RING[piece[1]]


def origin(half, piece):
    sz, sy = piece
    if half == 0:
        if sz == 0:
            return (0, 1) if sy in (1, 2) else (0, -1)
        if sz == 2:
            return (1, 0) if sy in (0, 1) else (-1, 0)
        return (1, 0) if sz == 1 else (-1, 0)
    if sy == 0:
        return (1, 0) if sz == 1 else (-1, 0)
    if sy == 2:
        return (0, 1) if sz in (0, 1) else (0, -1)
    return (0, 1) if sy == 1 else (0, -1)


def children(half, piece):
    found = []
    for other in PIECES:
        if other == (0, 0):
            continue
        ez, ey = origin(half, other)
        if ((other[0] - ez) % 4, (other[1] - ey) % 4) == piece:
            found.append(((-ez, -ey), other))
    return found


def place():
    dp, y, x = lax.axis_index("dp"), lax.axis_index("context"), lax.axis_index("tensor")
    return dp // 2, dp % 2, y, x


def shifted(z, c, y, x, dz=0, dy=0, dx=0):
    return (((z + dz + 4) % 4) * 2 + c, (y + dy + 4) % 4, (x + dx + 4) % 4)


def greet(devices):
    barrier = pltpu.get_barrier_semaphore()
    for device in devices:
        pl.semaphore_signal(barrier, inc=1, device_id=device, device_id_type=MESH)
    pl.semaphore_wait(barrier, len(devices))


def half_rows(half):
    return pl.ds(half * CUT, CUT)


def columns(start, size):
    return pl.ds(pl.multiple_of(start, size), size)


def gather_kernel(
    hidden, pw, dw, bias,
    w_out, h_out, proj, raw,
    W, H, acc, part,
    load_sem, hload_sem, hsend, hrecv, wsend, wrecv, psend, precv, wout_sem, hout_sem,
):
    z, c, y, x = place()
    other = 1 - c
    sibling = (z * 2 + other, y, x)

    def slot(piece):
        return ((z + piece[0]) % 4) * 4 + (y + piece[1]) % 4

    mine = slot((0, 0))
    loads = [
        pltpu.make_async_copy(pw, W.at[mine, pl.ds(0, 512)], load_sem.at[0]),
        pltpu.make_async_copy(dw, W.at[mine, pl.ds(512, 32)], load_sem.at[1]),
    ]
    for copy in loads:
        copy.start()
    hloads = []
    for k in range(4):
        copy = pltpu.make_async_copy(
            hidden.at[0, :, columns((2 * k + c) * 1024, 1024)],
            H.at[c, :, pl.ds(k * 1024, 1024)],
            hload_sem.at[k],
        )
        copy.start()
        hloads.append(copy)
    greet(
        [sibling]
        + [shifted(z, c, y, x, dz=s) for s in (1, -1)]
        + [shifted(z, c, y, x, dy=s) for s in (1, -1)]
    )
    for copy in loads:
        copy.wait()

    def relay(half, piece):
        started = []
        for (ez, ey), name in children(half, piece):
            index = slot(piece)
            copy = pltpu.make_async_remote_copy(
                src_ref=W.at[index, half_rows(half)],
                dst_ref=W.at[index, half_rows(half)],
                send_sem=wsend.at[half, name[0] * 4 + name[1]],
                recv_sem=wrecv.at[half, name[0] * 4 + name[1]],
                device_id=shifted(z, c, y, x, dz=ez, dy=ey),
                device_id_type=MESH,
            )
            copy.start()
            started.append(copy)
        return started

    def arrive(half, piece):
        index = slot(piece)
        pltpu.make_async_remote_copy(
            src_ref=W.at[index, half_rows(half)],
            dst_ref=W.at[index, half_rows(half)],
            send_sem=wsend.at[half, piece[0] * 4 + piece[1]],
            recv_sem=wrecv.at[half, piece[0] * 4 + piece[1]],
            device_id=sibling,
            device_id_type=MESH,
        ).wait_recv()

    sent = []
    for half in range(2):
        sent += relay(half, (0, 0))
    hremote = []
    for k in range(4):
        copy = pltpu.make_async_remote_copy(
            src_ref=hidden.at[0, :, columns((2 * k + other) * 1024, 1024)],
            dst_ref=H.at[c, :, pl.ds(k * 1024, 1024)],
            send_sem=hsend.at[k],
            recv_sem=hrecv.at[k],
            device_id=sibling,
            device_id_type=MESH,
        )
        copy.start()
        hremote.append(copy)
    acc[...] = jnp.zeros_like(acc)
    outs = []

    def multiply(piece):
        index = slot(piece)
        for r in range(2):
            acc[r] += lax.dot_general(
                H[r, :, columns(index * 256, 256)], W[index],
                (((1,), (1,)), ((), ())), preferred_element_type=f32,
            )
        copy = pltpu.make_async_copy(W.at[index], w_out.at[index], wout_sem.at[index])
        copy.start()
        outs.append(copy)

    for d in range(5):
        group = [p for p in PIECES if distance(p) == d]
        if d > 0:
            for piece in group:
                for half in range(2):
                    arrive(half, piece)
                    sent += relay(half, piece)
        if d == 1:
            for copy in hloads:
                copy.wait()
            for copy in hremote:
                copy.wait_recv()
            copy = pltpu.make_async_copy(H, h_out, hout_sem)
            copy.start()
            outs.append(copy)
            multiply((0, 0))
        if d > 0:
            for piece in group:
                multiply(piece)
    exchange = pltpu.make_async_remote_copy(
        src_ref=acc.at[other], dst_ref=part, send_sem=psend, recv_sem=precv,
        device_id=sibling, device_id_type=MESH,
    )
    exchange.start()
    exchange.wait_recv()
    total = acc[c] + part[...]
    proj[...] = total[:, :512].astype(bf16)
    raw[...] = total[:, 512:] + bias[...]
    exchange.wait_send()
    for copy in sent + hremote:
        copy.wait_send()
    for copy in outs:
        copy.wait()


VM = pl.BlockSpec(memory_space=pltpu.VMEM)
ANY = pl.BlockSpec(memory_space=pl.ANY)
DMA = pltpu.SemaphoreType.DMA


def gather_project(hidden, proj_weight, delta_weight, step_bias):
    return pl.pallas_call(
        gather_kernel,
        out_shape=(
            jax.ShapeDtypeStruct((16, ROWS, 256), bf16),
            jax.ShapeDtypeStruct((2, TOK, D // 2), bf16),
            jax.ShapeDtypeStruct((TOK, 512), bf16),
            jax.ShapeDtypeStruct((TOK, 32), f32),
        ),
        in_specs=[ANY, ANY, ANY, VM],
        out_specs=(ANY, ANY, VM, VM),
        scratch_shapes=[
            pltpu.VMEM((16, ROWS, 256), bf16),
            pltpu.VMEM((2, TOK, D // 2), bf16),
            pltpu.VMEM((2, TOK, ROWS), f32),
            pltpu.VMEM((TOK, ROWS), f32),
            DMA((2,)), DMA((4,)), DMA((4,)), DMA((4,)),
            DMA((2, 16)), DMA((2, 16)), DMA, DMA, DMA((16,)), DMA,
        ],
        compiler_params=pltpu.CompilerParams(
            collective_id=0, has_side_effects=True, vmem_limit_bytes=50 * 2**20
        ),
        name="gather_project",
    )(hidden, proj_weight, delta_weight, step_bias.reshape(1, 32))


def reduce_kernel(
    wr, small, w_in, h_in,
    hid_out, grad_out, small_out,
    W, H, WR, prod, sendbuf, rbuf, hpart, hown, xfar, xnear, res, sib_small, y_small, z_small,
    w_sem, h_sem, wr_sem, wrsend, wrrecv, xfsend, xfrecv, xnsend, xnrecv,
    gsend, grecv, rsend, rrecv, ssend, srecv,
):
    z, c, y, x = place()
    other = 1 - c
    sibling = (z * 2 + other, y, x)
    right, left = shifted(z, c, y, x, dx=1), shifted(z, c, y, x, dx=-1)

    def slot(piece):
        return ((z + piece[0]) % 4) * 4 + (y + piece[1]) % 4

    def remote(src, dst, send, recv, device):
        return pltpu.make_async_remote_copy(
            src_ref=src, dst_ref=dst, send_sem=send, recv_sem=recv,
            device_id=device, device_id_type=MESH,
        )

    wload = pltpu.make_async_copy(w_in, W, w_sem)
    wload.start()
    hload = pltpu.make_async_copy(h_in, H, h_sem)
    hload.start()
    wrload = pltpu.make_async_copy(wr, WR.at[c], wr_sem)
    wrload.start()
    greet(
        [sibling, right, left]
        + [shifted(z, c, y, x, dz=s) for s in (1, 2, 3)]
        + [shifted(z, c, y, x, dy=s) for s in (1, 2, 3)]
    )
    started = []

    def go(copy):
        copy.start()
        started.append(copy)
        return copy

    wr_copy = go(remote(wr, WR.at[c], wrsend, wrrecv, sibling))
    s_copy = go(remote(small, sib_small, ssend.at[0], srecv.at[0], sibling))
    wrload.wait()
    wr_copy.wait_recv()
    wload.wait()

    def hidden_chunk(offset, store):
        chunk = (x + offset) % 4
        for r in range(2):
            for k in range(4):
                value = jnp.dot(WR[r], W[chunk * 4 + k], preferred_element_type=f32)
                store(r, k, value)

    def to_part(index):
        def store(r, k, value):
            hpart[index, r, :, k * 256:(k + 1) * 256] = value.astype(bf16)
        return store

    def to_own(r, k, value):
        hown[r, :, k * 256:(k + 1) * 256] = value

    hidden_chunk(2, to_part(0))
    far_r = go(remote(hpart.at[0, 0], xfar.at[0], xfsend.at[0], xfrecv.at[0], right))
    far_l = go(remote(hpart.at[0, 1], xfar.at[1], xfsend.at[1], xfrecv.at[1], left))
    hidden_chunk(1, to_part(1))
    near_r1 = go(remote(hpart.at[1, 1], xnear.at[0, 1], xnsend.at[0, 1], xnrecv.at[0, 1], right))
    hidden_chunk(3, to_part(2))
    near_l0 = go(remote(hpart.at[2, 0], xnear.at[1, 0], xnsend.at[1, 0], xnrecv.at[1, 0], left))

    hload.wait()

    def rows_of(half):
        return slice(half * CUT, (half + 1) * CUT)

    def product(piece):
        index = slot(piece)
        k = piece[0] * 4 + piece[1]
        value = lax.dot_general(
            WR[0], H[0, :, columns(index * 256, 256)], (((0,), (0,)), ((), ())),
            preferred_element_type=f32,
        )
        value += lax.dot_general(
            WR[1], H[1, :, columns(index * 256, 256)], (((0,), (0,)), ((), ())),
            preferred_element_type=f32,
        )
        prod[k] = value

    def up(half, piece):
        k = piece[0] * 4 + piece[1]
        ez, ey = origin(half, piece)
        go(remote(
            sendbuf.at[k, half_rows(half)], rbuf.at[half, k],
            gsend.at[half, k], grecv.at[half, k], shifted(z, c, y, x, dz=ez, dy=ey),
        ))

    def total(half, piece):
        k = piece[0] * 4 + piece[1]
        value = prod[k, rows_of(half)]
        for _, name in children(half, piece):
            m = name[0] * 4 + name[1]
            remote(
                sendbuf.at[k, half_rows(half)], rbuf.at[half, m],
                gsend.at[half, m], grecv.at[half, m], sibling,
            ).wait_recv()
            value = value + rbuf[half, m].astype(f32)
        return value

    order = sorted(PIECES, key=lambda p: -distance(p))
    for piece in order:
        product(piece)
        for half in range(2):
            if piece != (0, 0) and not children(half, piece):
                sendbuf[piece[0] * 4 + piece[1], rows_of(half)] = prod[
                    piece[0] * 4 + piece[1], rows_of(half)
                ].astype(bf16)
                up(half, piece)

    s_copy.wait_recv()
    y_small[y] = small[...] + sib_small[...]
    y_copies = []
    for s in (1, 2, 3):
        y_copies.append(go(remote(
            y_small.at[y], y_small.at[y], ssend.at[s], srecv.at[s], shifted(z, c, y, x, dy=s)
        )))

    far_r.wait_recv()
    hpart[1, 0] = (hpart[1, 0].astype(f32) + xfar[0].astype(f32)).astype(bf16)
    near_r0 = go(remote(hpart.at[1, 0], xnear.at[0, 0], xnsend.at[0, 0], xnrecv.at[0, 0], right))
    far_l.wait_recv()
    hpart[2, 1] = (hpart[2, 1].astype(f32) + xfar[1].astype(f32)).astype(bf16)
    near_l1 = go(remote(hpart.at[2, 1], xnear.at[1, 1], xnsend.at[1, 1], xnrecv.at[1, 1], left))
    hidden_chunk(0, to_own)

    for s in (1, 2, 3):
        source = (y - s + 4) % 4
        remote(
            y_small.at[y], y_small.at[source], ssend.at[s], srecv.at[s], sibling
        ).wait_recv()
    z_small[z] = (y_small[0] + y_small[1]) + (y_small[2] + y_small[3])
    for s in (1, 2, 3):
        go(remote(
            z_small.at[z], z_small.at[z], ssend.at[3 + s], srecv.at[3 + s],
            shifted(z, c, y, x, dz=s),
        ))

    for d in (3, 2, 1):
        for piece in order:
            if distance(piece) != d:
                continue
            for half in range(2):
                if children(half, piece):
                    sendbuf[piece[0] * 4 + piece[1], rows_of(half)] = total(half, piece).astype(bf16)
                    up(half, piece)
    for half in range(2):
        grad_out[rows_of(half)] = total(half, (0, 0))

    for s in (1, 2, 3):
        source = (z - s + 4) % 4
        remote(
            z_small.at[z], z_small.at[source], ssend.at[3 + s], srecv.at[3 + s], sibling
        ).wait_recv()
    small_out[...] = (z_small[0] + z_small[1]) + (z_small[2] + z_small[3])

    def finish(r):
        return (hown[r] + xnear[0, r].astype(f32) + xnear[1, r].astype(f32)).astype(bf16)

    near_r1.wait_recv()
    near_l0.wait_recv()
    near_r0.wait_recv()
    near_l1.wait_recv()
    res[0] = finish(0)
    res[1] = finish(1)
    swap = go(remote(
        res.at[other], hid_out.at[:, columns(c * 1024, 1024)], rsend, rrecv, sibling
    ))
    hid_out[:, columns(c * 1024, 1024)] = res[c]
    swap.wait_recv()
    for copy in started:
        copy.wait_send()


def reduce_all(wr, small, w_all, h_all):
    return pl.pallas_call(
        reduce_kernel,
        out_shape=(
            jax.ShapeDtypeStruct((TOK, 2048), bf16),
            jax.ShapeDtypeStruct((ROWS, 256), f32),
            jax.ShapeDtypeStruct((8, 128), f32),
        ),
        in_specs=[VM, VM, ANY, ANY],
        out_specs=(VM, VM, VM),
        scratch_shapes=[
            pltpu.VMEM((16, ROWS, 256), bf16),
            pltpu.VMEM((2, TOK, D // 2), bf16),
            pltpu.VMEM((2, TOK, ROWS), bf16),
            pltpu.VMEM((16, ROWS, 256), f32),
            pltpu.VMEM((16, ROWS, 256), bf16),
            pltpu.VMEM((2, 16, CUT, 256), bf16),
            pltpu.VMEM((3, 2, TOK, 1024), bf16),
            pltpu.VMEM((2, TOK, 1024), f32),
            pltpu.VMEM((2, TOK, 1024), bf16),
            pltpu.VMEM((2, 2, TOK, 1024), bf16),
            pltpu.VMEM((2, TOK, 1024), bf16),
            pltpu.VMEM((8, 128), f32),
            pltpu.VMEM((4, 8, 128), f32),
            pltpu.VMEM((4, 8, 128), f32),
            DMA, DMA, DMA, DMA, DMA, DMA((2,)), DMA((2,)), DMA((2, 2)), DMA((2, 2)),
            DMA((2, 16)), DMA((2, 16)), DMA, DMA, DMA((7,)), DMA((7,)),
        ],
        compiler_params=pltpu.CompilerParams(
            collective_id=1, has_side_effects=True, vmem_limit_bytes=56 * 2**20
        ),
        name="reduce_gradients",
    )(wr, small, w_all, h_all)


def carried_in(value, axis, combine, identity, reverse):
    length, index = (lax.axis_size(axis), lax.axis_index(axis))
    everything = jax.tree.map(
        lambda part, kind: lax.all_gather(part.astype(kind), axis),
        value,
        (jnp.bfloat16, jnp.bfloat16),
    )
    start = jax.tree.map(
        lambda part, zero: jnp.broadcast_to(jnp.asarray(zero, part.dtype), part.shape),
        value,
        identity,
    )

    def step(k, before):
        at = length - 1 - k if reverse else k
        reached = at > index if reverse else at < index
        new = combine(
            before, jax.tree.map(lambda part, own: part[at].astype(own.dtype), everything, value)
        )
        return jax.tree.map(lambda a, b: jnp.where(reached, a, b), new, before)

    return lax.fori_loop(0, length, step, start)


def prepare(inputs, delta, writes, reads, decay_rate, start):
    tokens, heads, width = inputs.shape
    groups = writes.shape[1]
    per_group = heads // groups
    blocks = tokens // Q
    values = inputs.reshape(blocks, Q, groups, per_group, width)
    steps = jnp.transpose(delta.reshape(blocks, Q, groups, per_group), (0, 2, 3, 1))
    write_blocks = writes.reshape(blocks, Q, groups, -1)
    read_blocks = reads.reshape(blocks, Q, groups, -1)
    logs = jnp.cumsum(-decay_rate.reshape(1, groups, per_group, 1) * steps, axis=3)
    marks = jnp.cumsum(start.reshape(blocks, Q), axis=1)
    return (values, steps, write_blocks, read_blocks, logs, marks)


def state_terms(values, steps, write_blocks, logs, marks):
    same_doc = (marks[:, -1:] == marks)[:, None, None, :]
    tail = jnp.where(same_doc, jnp.exp(logs[..., -1:] - logs), 0.0)
    block_states = jnp.einsum(
        "cgjs,csgjp,csgn->cgjpn", tail * steps, values, write_blocks, precision=highest
    )
    keeps = jnp.where((marks[:, -1] == 0)[:, None, None], jnp.exp(logs[..., -1]), 0.0)
    return (keeps, block_states)


def ssd_forward(inputs, delta, writes, reads, decay_rate, start, state):
    tokens, heads, width = inputs.shape
    values, steps, write_blocks, read_blocks, logs, marks = prepare(
        inputs, delta, writes, reads, decay_rate, start
    )
    order = jnp.arange(Q, dtype=jnp.int32)
    inside = (order[:, None] >= order[None, :])[None] & (marks[:, :, None] == marks[:, None, :])
    inside = inside[:, None, None]
    gaps = jnp.where(inside, logs[..., :, None] - logs[..., None, :], 0.0)
    weights = jnp.where(inside, jnp.exp(gaps), 0.0)
    scores = jnp.einsum("ctgn,csgn->cgts", read_blocks, write_blocks, precision=highest)
    mixing = scores[:, :, None] * weights * steps[:, :, :, None, :]
    local_out = jnp.einsum("cgjts,csgjp->ctgjp", mixing, values, precision=highest)
    keeps, block_states = state_terms(values, steps, write_blocks, logs, marks)

    def advance(carry, pair):
        keep, block_state = pair
        return (keep[..., None, None] * carry + block_state, carry)

    final, entering = lax.scan(advance, state, (keeps, block_states))
    head = jnp.where((marks == 0)[:, None, None, :], jnp.exp(logs), 0.0)
    carried_out = jnp.einsum(
        "cgjt,cgjpn,ctgn->ctgjp", head, entering, read_blocks, precision=highest
    )
    total = local_out + carried_out
    return (total.reshape(tokens, heads, width), final)


def chain_terms(inputs, delta, writes, reads, decay_rate, start, grads_in):
    values, steps, write_blocks, read_blocks, logs, marks = prepare(
        inputs, delta, writes, reads, decay_rate, start
    )
    keeps, block_states = state_terms(values, steps, write_blocks, logs, marks)
    head = jnp.where((marks == 0)[:, None, None, :], jnp.exp(logs), 0.0)
    grad_blocks = grads_in.reshape(values.shape)
    ones = jnp.ones_like(keeps[:1])
    before = jnp.cumprod(jnp.concatenate([ones, keeps[:-1]], axis=0), axis=0)
    through = jnp.cumprod(keeps[::-1], axis=0)[::-1]
    after = jnp.concatenate([through[1:], ones], axis=0)
    front = jnp.sum(after[..., None, None] * block_states, axis=0)
    pulled = jnp.einsum("cgjt,ctgjp,ctgn->cgjpn", head, grad_blocks, read_blocks, precision=highest)
    back = jnp.sum(before[..., None, None] * pulled, axis=0)
    return (jnp.prod(keeps, axis=0), front, back)


def link(earlier, later):
    return (earlier[0] * later[0], later[1] + later[0][..., None, None] * earlier[1])


def adam_direction(grad, moment, second):
    moment = beta_one * moment + (1.0 - beta_one) * grad
    second = beta_two * second + (1.0 - beta_two) * grad * grad
    corrected = moment / (1.0 - beta_one**adam_step)
    return corrected / (jnp.sqrt(second / (1.0 - beta_two**adam_step)) + adam_eps)


def shards(
    hidden,
    inputs,
    upstream,
    proj_weight,
    delta_weight,
    decay_rate,
    step_bias,
    proj_moment,
    proj_second,
    delta_moment,
    delta_second,
    doc_lengths,
    valid_counts,
):
    tokens = hidden.shape[1]
    heads = decay_rate.shape[0]
    groups = proj_weight.shape[0] // (2 * N)
    w_all, h_all, projected, raw = gather_project(hidden, proj_weight, delta_weight, step_bias)
    projected = projected.astype(f32)
    mixed = projected.reshape(tokens, groups, 2, N)
    writes = mixed[:, :, 0]
    reads = mixed[:, :, 1]
    order = jnp.arange(tokens, dtype=jnp.int32)
    place = lax.axis_index("context") * tokens + order
    valid = jnp.where(order < valid_counts[0, 0], 1.0, 0.0).astype(jnp.float32)
    starts = jnp.cumsum(doc_lengths[0]) - doc_lengths[0]
    start = jnp.where(jnp.any(place[:, None] == starts[None, :], axis=1), 1.0, 0.0).astype(
        jnp.float32
    )
    delta = valid[:, None] * jax.nn.softplus(raw)
    values = inputs[0].astype(jnp.float32).reshape(tokens, heads, HEAD_DIM)
    grads_in = (
        upstream[0].astype(jnp.float32).reshape(tokens, heads, HEAD_DIM) * valid[:, None, None]
    )
    carried, front, back = chain_terms(values, delta, writes, reads, decay_rate, start, grads_in)
    identity = (jnp.ones_like(carried), jnp.zeros_like(front))
    state = carried_in((carried, front), "context", link, identity, False)[1]
    later = carried_in((carried, back), "context", link, identity, True)[1]

    def local(inputs_here, delta_here, writes_here, reads_here, rate_here):
        return ssd_forward(
            inputs_here, delta_here, writes_here, reads_here, rate_here, start, state
        )

    unused, pull = jax.vjp(local, values, delta, writes, reads, decay_rate)
    value_grad, delta_grad, write_grad, read_grad, rate_grad = pull((grads_in, later))
    raw_grad = delta_grad * valid[:, None] * jax.nn.sigmoid(raw)
    write_read = (
        jnp.stack([write_grad, read_grad], axis=2)
        .reshape(tokens, 2 * groups * N)
        .astype(jnp.bfloat16)
    )
    raw_round = raw_grad.astype(jnp.bfloat16)
    wr = jnp.concatenate([write_read, raw_round], axis=1)
    small = jnp.zeros((8, 128), f32)
    small = small.at[0, :heads].set(rate_grad).at[1, :heads].set(jnp.sum(raw_grad, axis=0))
    small = small.at[2].set(valid_counts[0, 0].astype(f32))
    hidden_grad, grads, sums = reduce_all(wr, small, w_all, h_all)
    hidden_grad = hidden_grad[None]
    proj_sum, delta_sum = grads[:512], grads[512:]
    head_sum, count_sum = sums[:2, :heads], sums[2, 0]
    input_grad = value_grad.reshape(1, tokens, heads * HEAD_DIM).astype(jnp.bfloat16)
    proj_update = adam_direction(proj_sum / count_sum, proj_moment, proj_second)
    delta_update = adam_direction(delta_sum / count_sum, delta_moment, delta_second)
    return (
        input_grad,
        hidden_grad,
        head_sum[0] / count_sum,
        head_sum[1] / count_sum,
        proj_update,
        delta_update,
    )


def solution(mesh):
    return jax.shard_map(
        shards,
        mesh=mesh,
        in_specs=(
            P("dp", "context", None),
            P("dp", "context", "tensor"),
            P("dp", "context", "tensor"),
            P("tensor", ("dp", "context")),
            P("tensor", ("dp", "context")),
            P("tensor"),
            P("tensor"),
            P("tensor", ("dp", "context")),
            P("tensor", ("dp", "context")),
            P("tensor", ("dp", "context")),
            P("tensor", ("dp", "context")),
            P("dp", None),
            P("dp", "context"),
        ),
        out_specs=(
            P("dp", "context", "tensor"),
            P("dp", "context", "tensor"),
            P("tensor"),
            P("tensor"),
            P("tensor", ("dp", "context")),
            P("tensor", ("dp", "context")),
        ),
        check_vma=False,
    )
```

```python
import jax
import jax.numpy as jnp
from jax import lax
from jax.experimental import pallas as pl
from jax.experimental.pallas import tpu as pltpu
from jax.sharding import PartitionSpec as P

N = 256
D = 8192
TOK = 256
ROWS = 544
CUT = 272
MESH = pl.DeviceIdType.MESH
f32 = jnp.float32
bf16 = jnp.bfloat16

beta_one = 0.9
beta_two = 0.95
adam_eps = 1e-08
adam_step = 100
highest = lax.Precision.HIGHEST

RING = (0, 1, 2, 1)
PIECES = [(i, j) for i in range(4) for j in range(4)]


def distance(piece):
    return RING[piece[0]] + RING[piece[1]]


def origin(half, piece):
    sz, sy = piece
    if half == 0:
        if sz == 0:
            return (0, 1) if sy in (1, 2) else (0, -1)
        if sz == 2:
            return (1, 0) if sy in (0, 1) else (-1, 0)
        return (1, 0) if sz == 1 else (-1, 0)
    if sy == 0:
        return (1, 0) if sz == 1 else (-1, 0)
    if sy == 2:
        return (0, 1) if sz in (0, 1) else (0, -1)
    return (0, 1) if sy == 1 else (0, -1)


def children(half, piece):
    found = []
    for other in PIECES:
        if other == (0, 0):
            continue
        ez, ey = origin(half, other)
        if ((other[0] - ez) % 4, (other[1] - ey) % 4) == piece:
            found.append(((-ez, -ey), other))
    return found


def place():
    dp, y, x = lax.axis_index("dp"), lax.axis_index("context"), lax.axis_index("tensor")
    return dp // 2, dp % 2, y, x


def shifted(z, c, y, x, dz=0, dy=0, dx=0):
    return (((z + dz + 4) % 4) * 2 + c, (y + dy + 4) % 4, (x + dx + 4) % 4)


def greet(devices):
    barrier = pltpu.get_barrier_semaphore()
    for device in devices:
        pl.semaphore_signal(barrier, inc=1, device_id=device, device_id_type=MESH)
    pl.semaphore_wait(barrier, len(devices))


def half_rows(half):
    return pl.ds(half * CUT, CUT)


def columns(start, size):
    return pl.ds(pl.multiple_of(start, size), size)


def gather_kernel(
    hidden, pw, dw, bias,
    w_out, h_out, proj, raw,
    W, H, acc, part,
    load_sem, hload_sem, hsend, hrecv, wsend, wrecv, psend, precv, wout_sem, hout_sem,
):
    z, c, y, x = place()
    other = 1 - c
    sibling = (z * 2 + other, y, x)

    def slot(piece):
        return ((z + piece[0]) % 4) * 4 + (y + piece[1]) % 4

    mine = slot((0, 0))
    loads = [
        pltpu.make_async_copy(pw, W.at[mine, pl.ds(0, 512)], load_sem.at[0]),
        pltpu.make_async_copy(dw, W.at[mine, pl.ds(512, 32)], load_sem.at[1]),
    ]
    for copy in loads:
        copy.start()
    hloads = []
    for k in range(4):
        copy = pltpu.make_async_copy(
            hidden.at[0, :, columns((2 * k + c) * 1024, 1024)],
            H.at[c, :, pl.ds(k * 1024, 1024)],
            hload_sem.at[k],
        )
        copy.start()
        hloads.append(copy)
    greet(
        [sibling]
        + [shifted(z, c, y, x, dz=s) for s in (1, -1)]
        + [shifted(z, c, y, x, dy=s) for s in (1, -1)]
    )
    for copy in loads:
        copy.wait()

    def relay(half, piece):
        started = []
        for (ez, ey), name in children(half, piece):
            index = slot(piece)
            copy = pltpu.make_async_remote_copy(
                src_ref=W.at[index, half_rows(half)],
                dst_ref=W.at[index, half_rows(half)],
                send_sem=wsend.at[half, name[0] * 4 + name[1]],
                recv_sem=wrecv.at[half, name[0] * 4 + name[1]],
                device_id=shifted(z, c, y, x, dz=ez, dy=ey),
                device_id_type=MESH,
            )
            copy.start()
            started.append(copy)
        return started

    def arrive(half, piece):
        index = slot(piece)
        pltpu.make_async_remote_copy(
            src_ref=W.at[index, half_rows(half)],
            dst_ref=W.at[index, half_rows(half)],
            send_sem=wsend.at[half, piece[0] * 4 + piece[1]],
            recv_sem=wrecv.at[half, piece[0] * 4 + piece[1]],
            device_id=sibling,
            device_id_type=MESH,
        ).wait_recv()

    sent = []
    for half in range(2):
        sent += relay(half, (0, 0))
    hremote = []
    for k in range(4):
        copy = pltpu.make_async_remote_copy(
            src_ref=hidden.at[0, :, columns((2 * k + other) * 1024, 1024)],
            dst_ref=H.at[c, :, pl.ds(k * 1024, 1024)],
            send_sem=hsend.at[k],
            recv_sem=hrecv.at[k],
            device_id=sibling,
            device_id_type=MESH,
        )
        copy.start()
        hremote.append(copy)
    acc[...] = jnp.zeros_like(acc)
    outs = []

    def multiply(piece):
        index = slot(piece)
        for r in range(2):
            acc[r] += lax.dot_general(
                H[r, :, columns(index * 256, 256)], W[index],
                (((1,), (1,)), ((), ())), preferred_element_type=f32,
            )
        copy = pltpu.make_async_copy(W.at[index], w_out.at[index], wout_sem.at[index])
        copy.start()
        outs.append(copy)

    for d in range(5):
        group = [p for p in PIECES if distance(p) == d]
        if d > 0:
            for piece in group:
                for half in range(2):
                    arrive(half, piece)
                    sent += relay(half, piece)
        if d == 1:
            for copy in hloads:
                copy.wait()
            for copy in hremote:
                copy.wait_recv()
            copy = pltpu.make_async_copy(H, h_out, hout_sem)
            copy.start()
            outs.append(copy)
            multiply((0, 0))
        if d > 0:
            for piece in group:
                multiply(piece)
    exchange = pltpu.make_async_remote_copy(
        src_ref=acc.at[other], dst_ref=part, send_sem=psend, recv_sem=precv,
        device_id=sibling, device_id_type=MESH,
    )
    exchange.start()
    exchange.wait_recv()
    total = acc[c] + part[...]
    proj[...] = total[:, :512].astype(bf16)
    raw[...] = total[:, 512:] + bias[...]
    exchange.wait_send()
    for copy in sent + hremote:
        copy.wait_send()
    for copy in outs:
        copy.wait()


VM = pl.BlockSpec(memory_space=pltpu.VMEM)
ANY = pl.BlockSpec(memory_space=pl.ANY)
DMA = pltpu.SemaphoreType.DMA


def gather_project(hidden, proj_weight, delta_weight, step_bias):
    return pl.pallas_call(
        gather_kernel,
        out_shape=(
            jax.ShapeDtypeStruct((16, ROWS, 256), bf16),
            jax.ShapeDtypeStruct((2, TOK, D // 2), bf16),
            jax.ShapeDtypeStruct((TOK, 512), bf16),
            jax.ShapeDtypeStruct((TOK, 32), f32),
        ),
        in_specs=[ANY, ANY, ANY, VM],
        out_specs=(ANY, ANY, VM, VM),
        scratch_shapes=[
            pltpu.VMEM((16, ROWS, 256), bf16),
            pltpu.VMEM((2, TOK, D // 2), bf16),
            pltpu.VMEM((2, TOK, ROWS), f32),
            pltpu.VMEM((TOK, ROWS), f32),
            DMA((2,)), DMA((4,)), DMA((4,)), DMA((4,)),
            DMA((2, 16)), DMA((2, 16)), DMA, DMA, DMA((16,)), DMA,
        ],
        compiler_params=pltpu.CompilerParams(
            collective_id=0, has_side_effects=True, vmem_limit_bytes=50 * 2**20
        ),
        name="gather_project",
    )(hidden, proj_weight, delta_weight, step_bias.reshape(1, 32))


def reduce_kernel(
    wr, small, w_in, h_in,
    hid_out, grad_out, small_out,
    W, H, WR, prod, sendbuf, rbuf, hpart, hown, xfar, xnear, res, sib_small, y_small, z_small,
    w_sem, h_sem, wr_sem, wrsend, wrrecv, xfsend, xfrecv, xnsend, xnrecv,
    gsend, grecv, rsend, rrecv, ssend, srecv,
):
    z, c, y, x = place()
    other = 1 - c
    sibling = (z * 2 + other, y, x)
    right, left = shifted(z, c, y, x, dx=1), shifted(z, c, y, x, dx=-1)

    def slot(piece):
        return ((z + piece[0]) % 4) * 4 + (y + piece[1]) % 4

    def remote(src, dst, send, recv, device):
        return pltpu.make_async_remote_copy(
            src_ref=src, dst_ref=dst, send_sem=send, recv_sem=recv,
            device_id=device, device_id_type=MESH,
        )

    wload = pltpu.make_async_copy(w_in, W, w_sem)
    wload.start()
    hload = pltpu.make_async_copy(h_in, H, h_sem)
    hload.start()
    wrload = pltpu.make_async_copy(wr, WR.at[c], wr_sem)
    wrload.start()
    greet(
        [sibling, right, left]
        + [shifted(z, c, y, x, dz=s) for s in (1, 2, 3)]
        + [shifted(z, c, y, x, dy=s) for s in (1, 2, 3)]
    )
    started = []

    def go(copy):
        copy.start()
        started.append(copy)
        return copy

    wr_copy = go(remote(wr, WR.at[c], wrsend, wrrecv, sibling))
    s_copy = go(remote(small, sib_small, ssend.at[0], srecv.at[0], sibling))
    wrload.wait()
    wr_copy.wait_recv()
    wload.wait()

    def hidden_chunk(offset, store):
        chunk = (x + offset) % 4
        for r in range(2):
            for k in range(4):
                value = jnp.dot(WR[r], W[chunk * 4 + k], preferred_element_type=f32)
                store(r, k, value)

    def to_part(index):
        def store(r, k, value):
            hpart[index, r, :, k * 256:(k + 1) * 256] = value.astype(bf16)
        return store

    def to_own(r, k, value):
        hown[r, :, k * 256:(k + 1) * 256] = value

    hidden_chunk(2, to_part(0))
    far_r = go(remote(hpart.at[0, 0], xfar.at[0], xfsend.at[0], xfrecv.at[0], right))
    far_l = go(remote(hpart.at[0, 1], xfar.at[1], xfsend.at[1], xfrecv.at[1], left))
    hidden_chunk(1, to_part(1))
    near_r1 = go(remote(hpart.at[1, 1], xnear.at[0, 1], xnsend.at[0, 1], xnrecv.at[0, 1], right))
    hidden_chunk(3, to_part(2))
    near_l0 = go(remote(hpart.at[2, 0], xnear.at[1, 0], xnsend.at[1, 0], xnrecv.at[1, 0], left))

    hload.wait()

    def rows_of(half):
        return slice(half * CUT, (half + 1) * CUT)

    def product(piece):
        index = slot(piece)
        k = piece[0] * 4 + piece[1]
        value = lax.dot_general(
            WR[0], H[0, :, columns(index * 256, 256)], (((0,), (0,)), ((), ())),
            preferred_element_type=f32,
        )
        value += lax.dot_general(
            WR[1], H[1, :, columns(index * 256, 256)], (((0,), (0,)), ((), ())),
            preferred_element_type=f32,
        )
        prod[k] = value

    def up(half, piece):
        k = piece[0] * 4 + piece[1]
        ez, ey = origin(half, piece)
        go(remote(
            sendbuf.at[k, half_rows(half)], rbuf.at[half, k],
            gsend.at[half, k], grecv.at[half, k], shifted(z, c, y, x, dz=ez, dy=ey),
        ))

    def total(half, piece):
        k = piece[0] * 4 + piece[1]
        value = prod[k, rows_of(half)]
        for _, name in children(half, piece):
            m = name[0] * 4 + name[1]
            remote(
                sendbuf.at[k, half_rows(half)], rbuf.at[half, m],
                gsend.at[half, m], grecv.at[half, m], sibling,
            ).wait_recv()
            value = value + rbuf[half, m].astype(f32)
        return value

    order = sorted(PIECES, key=lambda p: -distance(p))
    for piece in order:
        product(piece)
        for half in range(2):
            if piece != (0, 0) and not children(half, piece):
                sendbuf[piece[0] * 4 + piece[1], rows_of(half)] = prod[
                    piece[0] * 4 + piece[1], rows_of(half)
                ].astype(bf16)
                up(half, piece)

    s_copy.wait_recv()
    y_small[y] = small[...] + sib_small[...]
    y_copies = []
    for s in (1, 2, 3):
        y_copies.append(go(remote(
            y_small.at[y], y_small.at[y], ssend.at[s], srecv.at[s], shifted(z, c, y, x, dy=s)
        )))

    far_r.wait_recv()
    hpart[1, 0] = (hpart[1, 0].astype(f32) + xfar[0].astype(f32)).astype(bf16)
    near_r0 = go(remote(hpart.at[1, 0], xnear.at[0, 0], xnsend.at[0, 0], xnrecv.at[0, 0], right))
    far_l.wait_recv()
    hpart[2, 1] = (hpart[2, 1].astype(f32) + xfar[1].astype(f32)).astype(bf16)
    near_l1 = go(remote(hpart.at[2, 1], xnear.at[1, 1], xnsend.at[1, 1], xnrecv.at[1, 1], left))
    hidden_chunk(0, to_own)

    for s in (1, 2, 3):
        source = (y - s + 4) % 4
        remote(
            y_small.at[y], y_small.at[source], ssend.at[s], srecv.at[s], sibling
        ).wait_recv()
    z_small[z] = (y_small[0] + y_small[1]) + (y_small[2] + y_small[3])
    for s in (1, 2, 3):
        go(remote(
            z_small.at[z], z_small.at[z], ssend.at[3 + s], srecv.at[3 + s],
            shifted(z, c, y, x, dz=s),
        ))

    for d in (3, 2, 1):
        for piece in order:
            if distance(piece) != d:
                continue
            for half in range(2):
                if children(half, piece):
                    sendbuf[piece[0] * 4 + piece[1], rows_of(half)] = total(half, piece).astype(bf16)
                    up(half, piece)
    for half in range(2):
        grad_out[rows_of(half)] = total(half, (0, 0))

    for s in (1, 2, 3):
        source = (z - s + 4) % 4
        remote(
            z_small.at[z], z_small.at[source], ssend.at[3 + s], srecv.at[3 + s], sibling
        ).wait_recv()
    small_out[...] = (z_small[0] + z_small[1]) + (z_small[2] + z_small[3])

    def finish(r):
        return (hown[r] + xnear[0, r].astype(f32) + xnear[1, r].astype(f32)).astype(bf16)

    near_r1.wait_recv()
    near_l0.wait_recv()
    near_r0.wait_recv()
    near_l1.wait_recv()
    res[0] = finish(0)
    res[1] = finish(1)
    swap = go(remote(
        res.at[other], hid_out.at[:, columns(c * 1024, 1024)], rsend, rrecv, sibling
    ))
    hid_out[:, columns(c * 1024, 1024)] = res[c]
    swap.wait_recv()
    for copy in started:
        copy.wait_send()


def reduce_all(wr, small, w_all, h_all):
    return pl.pallas_call(
        reduce_kernel,
        out_shape=(
            jax.ShapeDtypeStruct((TOK, 2048), bf16),
            jax.ShapeDtypeStruct((ROWS, 256), f32),
            jax.ShapeDtypeStruct((32, 128), f32),
        ),
        in_specs=[VM, VM, ANY, ANY],
        out_specs=(VM, VM, VM),
        scratch_shapes=[
            pltpu.VMEM((16, ROWS, 256), bf16),
            pltpu.VMEM((2, TOK, D // 2), bf16),
            pltpu.VMEM((2, TOK, ROWS), bf16),
            pltpu.VMEM((16, ROWS, 256), f32),
            pltpu.VMEM((16, ROWS, 256), bf16),
            pltpu.VMEM((2, 16, CUT, 256), bf16),
            pltpu.VMEM((3, 2, TOK, 1024), bf16),
            pltpu.VMEM((2, TOK, 1024), f32),
            pltpu.VMEM((2, TOK, 1024), bf16),
            pltpu.VMEM((2, 2, TOK, 1024), bf16),
            pltpu.VMEM((2, TOK, 1024), bf16),
            pltpu.VMEM((32, 128), f32),
            pltpu.VMEM((4, 32, 128), f32),
            pltpu.VMEM((4, 32, 128), f32),
            DMA, DMA, DMA, DMA, DMA, DMA((2,)), DMA((2,)), DMA((2, 2)), DMA((2, 2)),
            DMA((2, 16)), DMA((2, 16)), DMA, DMA, DMA((7,)), DMA((7,)),
        ],
        compiler_params=pltpu.CompilerParams(
            collective_id=1, has_side_effects=True, vmem_limit_bytes=56 * 2**20
        ),
        name="reduce_gradients",
    )(wr, small, w_all, h_all)


def scan_kernel(
    x_in, g_in, projected, raw, rate, docs, counts,
    wr, dx, small,
    XT, GT, A, FB, zin, zmsg, UV, Y, bias, score, dscore, dvec, vec,
    delta_s, tail_s, head_s, logs_s, keep_s, td_s, lcol, rcol, csum, qsum, xvsum, gusum, lsum,
    ssem, rsem,
):
    z, c, y, x = place()
    greet([shifted(z, c, y, x, dy=s) for s in (1, -1)])
    near = y // 2
    far = 1 - near
    inner = (y == 1) | (y == 2)

    def onward(way):
        return shifted(z, c, y, x, dy=1 - 2 * way)

    base = y * TOK
    count = counts[0, 0]
    starts = []
    at = jnp.int32(0)
    for k in range(4):
        starts.append(at)
        at = at + docs[0, k]

    def marks(position):
        total = jnp.zeros(position.shape, jnp.int32)
        for s in starts:
            total = total + jnp.where((s >= base) & (position >= s - base), 1, 0)
        return total

    tok_row = lax.broadcasted_iota(jnp.int32, (32, TOK), 1)
    marks_row = marks(tok_row)
    marks_last = marks(jnp.full((32, TOK), TOK - 1, jnp.int32))
    valid_row = jnp.where(tok_row < count, 1.0, 0.0).astype(f32)
    t_at = lax.broadcasted_iota(jnp.int32, (TOK, TOK), 0)
    s_at = lax.broadcasted_iota(jnp.int32, (TOK, TOK), 1)
    inside = (t_at >= s_at) & (marks(t_at) == marks(s_at)) & (t_at < count)
    bias[...] = jnp.where(inside, 0.0, -1e30).astype(f32)
    up_to = jnp.where(t_at <= s_at, 1.0, 0.0).astype(f32)
    down_to = jnp.where(t_at >= s_at, 1.0, 0.0).astype(f32)

    raw_t = raw[...].T
    delta = valid_row * (jnp.maximum(raw_t, 0.0) + jnp.log1p(jnp.exp(-jnp.abs(raw_t))))
    logs = jnp.dot(-rate[...] * delta, up_to, precision=highest, preferred_element_type=f32)
    last = logs[:, TOK - 1:TOK]
    tail = jnp.where(marks_row == marks_last, jnp.exp(last - logs), 0.0)
    head = jnp.where(marks_row == 0, jnp.exp(logs), 0.0) * valid_row
    keep = jnp.where(marks_last == 0, jnp.exp(jnp.broadcast_to(last, (32, TOK))), 0.0)
    delta_s[...] = delta
    tail_s[...] = tail
    head_s[...] = head
    logs_s[...] = logs
    keep_s[...] = keep
    td_s[...] = tail * delta
    logs_col = logs.T
    for i in range(8):
        lcol[i] = logs_col[:, 4 * i:4 * i + 4]
    writes, reads = projected[:, 0:N], projected[:, N:2 * N]
    vec[0] = reads
    vec[1] = writes
    dvec[...] = jnp.zeros_like(dvec)
    dscore[...] = jnp.zeros_like(dscore)

    @pl.when(jnp.logical_not(inner))
    def _():
        zin[near] = jnp.zeros((8, 256, N), bf16)
        UV[near] = jnp.zeros((8, 256, TOK), f32)

    def send(way, i):
        return pltpu.make_async_remote_copy(
            src_ref=zmsg.at[way, i], dst_ref=zin.at[way, i],
            send_sem=ssem.at[way, i], recv_sem=rsem.at[way, i],
            device_id=onward(way), device_id_type=MESH,
        )

    def ends(i, _):
        for pair in range(2):
            cols = pl.ds(pl.multiple_of(i * 256 + pair * 128, 128), 128)
            XT[i, pair * 128:(pair + 1) * 128, :] = x_in[0, :, cols].T
            GT[i, pair * 128:(pair + 1) * 128, :] = g_in[0, :, cols].T
        for j in range(4):
            r = slice(j * 64, (j + 1) * 64)
            h = pl.ds(4 * i + j, 1)
            A[0, i, r, :] = (GT[i, r, :].astype(f32) * head_s[h, :]).astype(bf16)
            A[1, i, r, :] = (XT[i, r, :].astype(f32) * td_s[h, :]).astype(bf16)
        FB[0, i] = jnp.dot(A[1, i], writes, preferred_element_type=f32)
        FB[1, i] = jnp.dot(A[0, i], reads, preferred_element_type=f32)

        @pl.when(jnp.logical_not(inner))
        def _():
            zmsg[near, i] = FB[near, i].astype(bf16)
            send(near, i).start()

        return 0

    lax.fori_loop(0, 8, ends, 0)
    score[...] = lax.dot_general(
        reads, writes, (((1,), (1,)), ((), ())), preferred_element_type=f32
    )

    def local(i):
        for pair in range(2):
            cols = pl.ds(pl.multiple_of(i * 256 + pair * 128, 128), 128)
            zero = jnp.zeros((64, TOK), bf16)
            for own in range(2):
                j = pair * 2 + own
                r = slice(j * 64, (j + 1) * 64)
                h = pl.ds(4 * i + j, 1)
                xh = XT[i, r, :]
                xm = jnp.concatenate([xh, zero] if own == 0 else [zero, xh], axis=0)
                lrow, drow = logs_s[h, :], delta_s[h, :]
                sums = None
                grads = None
                for t0, width in ((128, 256), (0, 128)):
                    t = slice(t0, t0 + 128)
                    gap = lcol[i, t, j:j + 1] - lrow[:, :width] + bias[t, :width]
                    decay = jnp.exp(gap)
                    dm = jnp.dot(g_in[0, t, cols], xm[:, :width], preferred_element_type=f32)
                    pulled = dm * decay * drow[:, :width]
                    dscore[t, :width] += pulled
                    sc = score[t, :width]
                    e = pulled * sc
                    rcol[i, t, j:j + 1] = jnp.sum(e, axis=1, keepdims=True)
                    es = jnp.sum(e, axis=0, keepdims=True)
                    mixed = jnp.dot(
                        GT[i, r, t], (sc * decay).astype(bf16), preferred_element_type=f32
                    )
                    if t0:
                        sums, grads = es, mixed
                        Y[i, r, 128:] = mixed[:, 128:]
                    else:
                        csum[h, :] = jnp.concatenate([sums[:, :128] + es, sums[:, 128:]], axis=1)
                        Y[i, r, :128] = grads[:, :128] + mixed

    def forward(way, i):
        for j in range(4):
            r = slice(j * 64, (j + 1) * 64)
            h = pl.ds(4 * i + j, 1)
            zmsg[way, i, r, :] = (
                FB[way, i, r, :] + keep_s[h, :] * zin[way, i, r, :].astype(f32)
            ).astype(bf16)
        send(way, i).start()

    def state_terms(way, i):
        state = zin[way, i]
        UV[way, i] = lax.dot_general(
            state, vec[way], (((1,), (1,)), ((), ())), preferred_element_type=f32
        )
        dvec[way] += lax.dot_general(
            A[way, i], state, (((0,), (0,)), ((), ())), preferred_element_type=f32
        )

    def finish(i):
        for pair in range(2):
            for own in range(2):
                j = pair * 2 + own
                r = slice(j * 64, (j + 1) * 64)
                h = pl.ds(4 * i + j, 1)
                v = UV[1, i, r, :]
                xt = XT[i, r, :].astype(f32)
                yt = Y[i, r, :] + tail_s[h, :] * v
                qsum[h, :] = jnp.sum(xt * yt, axis=0, keepdims=True)
                xvsum[h, :] = jnp.sum(xt * v, axis=0, keepdims=True)
                gusum[h, :] = jnp.sum(GT[i, r, :].astype(f32) * UV[0, i, r, :], axis=0, keepdims=True)
                lsum[h, :] = jnp.sum(
                    zin[0, i, r, :].astype(f32) * zin[1, i, r, :].astype(f32), axis=0, keepdims=True
                )
                Y[i, r, :] = delta_s[h, :] * yt
            cols = pl.ds(pl.multiple_of(i * 256 + pair * 128, 128), 128)
            dx[:, cols] = Y[i, pair * 128:(pair + 1) * 128, :].astype(bf16).T

    def step(k, _):
        @pl.when(k < 8)
        def _():
            local(k)

            @pl.when(inner)
            def _():
                send(near, k).wait_recv()
                forward(near, k)
                state_terms(near, k)

        @pl.when(k >= 2)
        def _():
            i = k - 2
            send(far, i).wait_recv()

            @pl.when(inner)
            def _():
                forward(far, i)

            state_terms(far, i)
            finish(i)

        return 0

    lax.fori_loop(0, 10, step, 0)

    rows = jnp.concatenate([rcol[i] for i in range(8)], axis=1).T
    pulls = td_s[...] * xvsum[...]
    change = rows - csum[...] + head_s[...] * gusum[...] - pulls
    at_end = jnp.sum(pulls + keep_s[...] * lsum[...], axis=1, keepdims=True)
    change = change + jnp.where(tok_row == TOK - 1, at_end, 0.0)
    dlog = jnp.dot(change, down_to, precision=highest, preferred_element_type=f32)
    ddelta = qsum[...] - rate[...] * dlog
    raw_t = raw[...].T
    valid_row = jnp.where(tok_row < count, 1.0, 0.0).astype(f32)
    raw_grad = ddelta * valid_row * (1.0 / (1.0 + jnp.exp(-raw_t)))
    rate_grad = jnp.sum(-delta_s[...] * dlog, axis=1, keepdims=True)
    bias_grad = jnp.sum(raw_grad, axis=1, keepdims=True)
    lane = lax.broadcasted_iota(jnp.int32, (32, 128), 1)
    small[...] = jnp.where(
        lane == 0, rate_grad, jnp.where(lane == 1, bias_grad, count.astype(f32))
    )
    ds = dscore[...].astype(bf16)
    wr[:, 0:N] = (
        dvec[1]
        + lax.dot_general(ds, vec[0], (((0,), (0,)), ((), ())), preferred_element_type=f32)
    ).astype(bf16)
    wr[:, N:2 * N] = (dvec[0] + jnp.dot(ds, vec[1], preferred_element_type=f32)).astype(bf16)
    wr[:, 2 * N:] = raw_grad.T.astype(bf16)

    def drain(i, _):
        send(near, i).wait_send()

        @pl.when(inner)
        def _():
            send(far, i).wait_send()

        return 0

    lax.fori_loop(0, 8, drain, 0)


def scan_states(inputs, upstream, projected, raw, decay_rate, doc_lengths, valid_counts):
    smem = pl.BlockSpec(memory_space=pltpu.SMEM)
    row = pltpu.VMEM((32, TOK), f32)
    return pl.pallas_call(
        scan_kernel,
        out_shape=(
            jax.ShapeDtypeStruct((TOK, ROWS), bf16),
            jax.ShapeDtypeStruct((TOK, 2048), bf16),
            jax.ShapeDtypeStruct((32, 128), f32),
        ),
        in_specs=[VM, VM, VM, VM, VM, smem, smem],
        out_specs=(VM, VM, VM),
        scratch_shapes=[
            pltpu.VMEM((8, 256, TOK), bf16),
            pltpu.VMEM((8, 256, TOK), bf16),
            pltpu.VMEM((2, 8, 256, TOK), bf16),
            pltpu.VMEM((2, 8, 256, N), f32),
            pltpu.VMEM((2, 8, 256, N), bf16),
            pltpu.VMEM((2, 8, 256, N), bf16),
            pltpu.VMEM((2, 8, 256, TOK), f32),
            pltpu.VMEM((8, 256, TOK), f32),
            pltpu.VMEM((TOK, TOK), f32),
            pltpu.VMEM((TOK, TOK), f32),
            pltpu.VMEM((TOK, TOK), f32),
            pltpu.VMEM((2, TOK, N), f32),
            pltpu.VMEM((2, TOK, N), bf16),
            row, row, row, row, row, row,
            pltpu.VMEM((8, TOK, 4), f32),
            pltpu.VMEM((8, TOK, 4), f32),
            row, row, row, row, row,
            DMA((2, 8)), DMA((2, 8)),
        ],
        compiler_params=pltpu.CompilerParams(
            collective_id=2, has_side_effects=True, vmem_limit_bytes=50 * 2**20
        ),
        name="scan_states",
    )(inputs, upstream, projected, raw, decay_rate.reshape(32, 1), doc_lengths, valid_counts)


def adam_direction(grad, moment, second):
    moment = beta_one * moment + (1.0 - beta_one) * grad
    second = beta_two * second + (1.0 - beta_two) * grad * grad
    corrected = moment / (1.0 - beta_one**adam_step)
    return corrected / (jnp.sqrt(second / (1.0 - beta_two**adam_step)) + adam_eps)


def shards(
    hidden,
    inputs,
    upstream,
    proj_weight,
    delta_weight,
    decay_rate,
    step_bias,
    proj_moment,
    proj_second,
    delta_moment,
    delta_second,
    doc_lengths,
    valid_counts,
):
    w_all, h_all, projected, raw = gather_project(hidden, proj_weight, delta_weight, step_bias)
    wr, input_grad, small = scan_states(
        inputs, upstream, projected, raw, decay_rate, doc_lengths, valid_counts
    )
    hidden_grad, grads, sums = reduce_all(wr, small, w_all, h_all)
    proj_sum, delta_sum = grads[:512], grads[512:]
    rate_sum, bias_sum, count_sum = sums[:, 0], sums[:, 1], sums[0, 2]
    proj_update = adam_direction(proj_sum / count_sum, proj_moment, proj_second)
    delta_update = adam_direction(delta_sum / count_sum, delta_moment, delta_second)
    return (
        input_grad[None],
        hidden_grad[None],
        rate_sum / count_sum,
        bias_sum / count_sum,
        proj_update,
        delta_update,
    )


def solution(mesh):
    return jax.shard_map(
        shards,
        mesh=mesh,
        in_specs=(
            P("dp", "context", None),
            P("dp", "context", "tensor"),
            P("dp", "context", "tensor"),
            P("tensor", ("dp", "context")),
            P("tensor", ("dp", "context")),
            P("tensor"),
            P("tensor"),
            P("tensor", ("dp", "context")),
            P("tensor", ("dp", "context")),
            P("tensor", ("dp", "context")),
            P("tensor", ("dp", "context")),
            P("dp", None),
            P("dp", "context"),
        ),
        out_specs=(
            P("dp", "context", "tensor"),
            P("dp", "context", "tensor"),
            P("tensor"),
            P("tensor"),
            P("tensor", ("dp", "context")),
            P("tensor", ("dp", "context")),
        ),
        check_vma=False,
    )
```

```python
import jax
import jax.numpy as jnp
from jax import lax
from jax.experimental import pallas as pl
from jax.experimental.pallas import tpu as pltpu
from jax.sharding import PartitionSpec as P

N = 256
D = 8192
TOK = 256
ROWS = 544
CUT = 272
ORDER = (
    (1, 4), (0, 1), (0, 3), (1, 12), (0, 4), (1, 1),
    (1, 3), (0, 12), (0, 5), (1, 5), (1, 7), (0, 13),
    (0, 7), (0, 2), (1, 15), (0, 15), (0, 8), (1, 13),
    (1, 8), (1, 14), (0, 9), (1, 2), (0, 14), (1, 11),
    (0, 6), (1, 6), (0, 11), (1, 10), (1, 9), (0, 10),
)
MESH = pl.DeviceIdType.MESH
f32 = jnp.float32
bf16 = jnp.bfloat16

beta_one = 0.9
beta_two = 0.95
adam_eps = 1e-08
adam_step = 100
highest = lax.Precision.HIGHEST

HPC = 4
LAG = 2
CH = 32 // HPC
CR = HPC * 64
PIECES = [(i, j) for i in range(4) for j in range(4)]


def origin(half, piece):
    sz, sy = piece
    if half == 0:
        if sz == 0:
            return (0, 1) if sy in (1, 2) else (0, -1)
        if sz == 2:
            return (1, 0) if sy in (0, 1) else (-1, 0)
        return (1, 0) if sz == 1 else (-1, 0)
    if sy == 0:
        return (1, 0) if sz == 1 else (-1, 0)
    if sy == 2:
        return (0, 1) if sz in (0, 1) else (0, -1)
    return (0, 1) if sy == 1 else (0, -1)


def children(half, piece):
    found = []
    for other in PIECES:
        if other == (0, 0):
            continue
        ez, ey = origin(half, other)
        if ((other[0] - ez) % 4, (other[1] - ey) % 4) == piece:
            found.append(((-ez, -ey), other))
    return found


def place():
    dp, y, x = lax.axis_index("dp"), lax.axis_index("context"), lax.axis_index("tensor")
    return dp // 2, dp % 2, y, x


def shifted(z, c, y, x, dz=0, dy=0, dx=0):
    return (((z + dz + 4) % 4) * 2 + c, (y + dy + 4) % 4, (x + dx + 4) % 4)


def greet(devices):
    barrier = pltpu.get_barrier_semaphore()
    for device in devices:
        pl.semaphore_signal(barrier, inc=1, device_id=device, device_id_type=MESH)
    pl.semaphore_wait(barrier, len(devices))


def half_rows(half):
    return pl.ds(half * CUT, CUT)


def columns(start, size):
    return pl.ds(pl.multiple_of(start, size), size)


def row_half(half):
    return slice(half * CUT, (half + 1) * CUT)


def rows_at(start, size):
    return pl.ds(pl.multiple_of(start, size), size)


def adam_direction(grad, moment, second):
    moment = beta_one * moment + (1.0 - beta_one) * grad
    second = beta_two * second + (1.0 - beta_two) * grad * grad
    corrected = moment / (1.0 - beta_one**adam_step)
    return corrected / (jnp.sqrt(second / (1.0 - beta_two**adam_step)) + adam_eps)


def layer_kernel(
    hidden, inputs, upstream, pw, dw, rate, step_bias, pm, ps, dmo, dse, docs, counts,
    dx_out, hid_out, pu_out, du_out, small_out,
    W, H, WX, acc, part, projected, raw, x_in, g_in, mom, sec,
    XT, GT, A, FB, zin, UV, Y, dx, mask, score, dscore, dvec, vec,
    delta_s, tail_s, head_s, logs_s, keep_s, td_s, lcol, rcol, csum, qsum, xvsum, gusum, lsum,
    WRX, sendbuf, rbuf, small, sib_small, y_small, z_small,
    load_sem, hload_sem, hsend, hrecv, wsend, wrecv, psend, precv, xsend, xrecv, in_sem, m_sem,
    ssem, rsem, dx_sem, wxsend, wxrecv, fsend, frecv, gsend, grecv, rsend, rrecv, csend, crecv,
):
    z, c, y, x = place()
    other = 1 - c
    sibling = (z * 2 + other, y, x)

    def remote(src, dst, send_sem, recv_sem, device):
        return pltpu.make_async_remote_copy(
            src_ref=src, dst_ref=dst, send_sem=send_sem, recv_sem=recv_sem,
            device_id=device, device_id_type=MESH,
        )

    started = []

    def go(copy):
        copy.start()
        started.append(copy)
        return copy

    def slot(piece):
        return ((z + piece[0]) % 4) * 4 + (y + piece[1]) % 4

    mine = slot((0, 0))
    loads = [
        pltpu.make_async_copy(pw, W.at[mine, pl.ds(0, 512)], load_sem.at[0]),
        pltpu.make_async_copy(dw, W.at[mine, pl.ds(512, 32)], load_sem.at[1]),
    ]
    hloads = [
        pltpu.make_async_copy(
            hidden.at[0, :, columns((2 * k + c) * 1024, 1024)],
            H.at[c, :, pl.ds(k * 1024, 1024)],
            hload_sem.at[k],
        )
        for k in range(4)
    ]
    in_loads = [
        pltpu.make_async_copy(inputs.at[0], x_in, in_sem.at[0]),
        pltpu.make_async_copy(upstream.at[0], g_in, in_sem.at[1]),
    ]
    m_loads = [
        pltpu.make_async_copy(pm, mom.at[pl.ds(0, 512)], m_sem.at[0]),
        pltpu.make_async_copy(dmo, mom.at[pl.ds(512, 32)], m_sem.at[1]),
        pltpu.make_async_copy(ps, sec.at[pl.ds(0, 512)], m_sem.at[2]),
        pltpu.make_async_copy(dse, sec.at[pl.ds(512, 32)], m_sem.at[3]),
    ]
    for copy in loads + hloads + in_loads + m_loads:
        copy.start()
    greet(
        [sibling]
        + [shifted(z, c, y, x, dz=s) for s in (1, 2, 3)]
        + [shifted(z, c, y, x, dy=s) for s in (1, 2, 3)]
        + [shifted(z, c, y, x, dx=s) for s in (1, 2, 3)]
    )
    for copy in loads:
        copy.wait()

    def gathered(half, index, name, device):
        part_ref = W.at[index, half_rows(half)]
        m = name[0] * 4 + name[1]
        return remote(part_ref, part_ref, wsend.at[half, m], wrecv.at[half, m], device)

    def relay(half, piece, axis=None):
        for (ez, ey), name in children(half, piece):
            if axis is None or (axis == 0) == (ez != 0):
                go(gathered(half, slot(piece), name, shifted(z, c, y, x, dz=ez, dy=ey)))

    def across(index, source, group):
        return remote(
            W.at[index], WX.at[source, index % 4],
            xsend.at[index], xrecv.at[source, index % 4], (z * 2 + c, y, group),
        )

    def complete(piece):
        index = slot(piece)
        group = (z + piece[0]) % 4

        @pl.when(group != x)
        def _():
            across(index, x, group).start()

    def multiply(piece):
        index = slot(piece)
        for r in range(2):
            acc[r] += lax.dot_general(
                H[r, :, columns(index * 256, 256)], W[index],
                (((1,), (1,)), ((), ())), preferred_element_type=f32,
            )

    relay(0, (0, 0), 1)
    relay(1, (0, 0), 0)
    relay(0, (0, 0), 0)
    relay(1, (0, 0), 1)
    hremote = []
    for k in range(4):
        hremote.append(go(remote(
            hidden.at[0, :, columns((2 * k + other) * 1024, 1024)],
            H.at[c, :, pl.ds(k * 1024, 1024)], hsend.at[k], hrecv.at[k], sibling,
        )))
    complete((0, 0))
    acc[...] = jnp.zeros_like(acc)
    for copy in in_loads:
        copy.wait()

    base = y * TOK
    count = counts[0, 0]
    starts = []
    at = jnp.int32(0)
    for k in range(4):
        starts.append(at)
        at = at + docs[0, k]

    def marks(position):
        total = jnp.zeros(position.shape, jnp.int32)
        for s in starts:
            total = total + jnp.where((s >= base) & (position >= s - base), 1, 0)
        return total

    tok_row = lax.broadcasted_iota(jnp.int32, (32, TOK), 1)
    t_at = lax.broadcasted_iota(jnp.int32, (TOK, TOK), 0)
    s_at = lax.broadcasted_iota(jnp.int32, (TOK, TOK), 1)
    inside = (t_at >= s_at) & (marks(t_at) == marks(s_at)) & (t_at < count)
    mask[...] = jnp.where(inside, 0.0, -1e30).astype(f32)

    def turn(p, _):
        cols = columns(p * 128, 128)
        XT[rows_at(p * 128, 128), :] = x_in[:, cols].T
        GT[rows_at(p * 128, 128), :] = g_in[:, cols].T
        return 0

    lax.fori_loop(0, 16, turn, 0)
    dvec[...] = jnp.zeros_like(dvec)
    dscore[...] = jnp.zeros_like(dscore)
    near = y // 2
    far = 1 - near
    inner = (y == 1) | (y == 2)

    @pl.when(jnp.logical_not(inner))
    def _():
        zin[near] = jnp.zeros((2048, N), bf16)
        UV[near] = jnp.zeros((2048, TOK), f32)

    seen = {}
    ready = False
    for half, m in ORDER:
        piece = (m // 4, m % 4)
        gathered(half, slot(piece), piece, sibling).wait_recv()
        relay(half, piece)
        seen[m] = seen.get(m, 0) + 1
        if seen[m] == 2:
            complete(piece)
            if not ready:
                for copy in hloads:
                    copy.wait()
                for copy in hremote:
                    copy.wait_recv()
                multiply((0, 0))
                ready = True
            multiply(piece)
    exchange = go(remote(acc.at[other], part, psend, precv, sibling))
    exchange.wait_recv()
    total_acc = acc[c] + part[...]
    projected[...] = total_acc[:, :512].astype(bf16)
    raw[...] = total_acc[:, 512:] + step_bias[...]

    def onward(way):
        return shifted(z, c, y, x, dy=1 - 2 * way)

    marks_row = marks(tok_row)
    marks_last = marks(jnp.full((32, TOK), TOK - 1, jnp.int32))
    valid_row = jnp.where(tok_row < count, 1.0, 0.0).astype(f32)
    up_to = jnp.where(t_at <= s_at, 1.0, 0.0).astype(f32)
    raw_t = raw[...].T
    delta = valid_row * (jnp.maximum(raw_t, 0.0) + jnp.log1p(jnp.exp(-jnp.abs(raw_t))))
    logs = jnp.dot(-rate[...] * delta, up_to, precision=highest, preferred_element_type=f32)
    last = logs[:, TOK - 1:TOK]
    tail = jnp.where(marks_row == marks_last, jnp.exp(last - logs), 0.0)
    head = jnp.where(marks_row == 0, jnp.exp(logs), 0.0) * valid_row
    keep = jnp.where(marks_last == 0, jnp.exp(jnp.broadcast_to(last, (32, TOK))), 0.0)
    delta_s[...] = delta
    tail_s[...] = tail
    head_s[...] = head
    logs_s[...] = logs
    keep_s[...] = keep
    td_s[...] = tail * delta
    writes, reads = projected[:, 0:N], projected[:, N:2 * N]
    vec[0] = reads
    vec[1] = writes

    def send(way, i):
        return remote(
            FB.at[way, rows_at(i * CR, CR)], zin.at[way, rows_at(i * CR, CR)],
            ssem.at[way, i], rsem.at[way, i], onward(way),
        )

    def ends(i, _):
        for j in range(HPC):
            r = rows_at(i * CR + j * 64, 64)
            h = pl.ds(HPC * i + j, 1)
            A[0, r, :] = (GT[r, :].astype(f32) * head_s[h, :]).astype(bf16)
            A[1, r, :] = (XT[r, :].astype(f32) * td_s[h, :]).astype(bf16)
        rc = rows_at(i * CR, CR)
        FB[0, rc, :] = jnp.dot(A[1, rc, :], writes, preferred_element_type=f32).astype(bf16)
        FB[1, rc, :] = jnp.dot(A[0, rc, :], reads, preferred_element_type=f32).astype(bf16)

        @pl.when(jnp.logical_not(inner))
        def _():
            send(near, i).start()

        return 0

    lax.fori_loop(0, CH, ends, 0)
    logs_col = logs.T
    for i in range(CH):
        lcol[i] = logs_col[:, HPC * i:HPC * i + HPC]
    score[...] = lax.dot_general(
        reads, writes, (((1,), (1,)), ((), ())), preferred_element_type=f32
    )

    def local(i):
        for pair in range(HPC // 2):
            cols = columns(i * CR + pair * 128, 128)
            zero = jnp.zeros((64, TOK), bf16)
            for own in range(2):
                j = pair * 2 + own
                r = rows_at(i * CR + j * 64, 64)
                h = pl.ds(HPC * i + j, 1)
                xh = XT[r, :]
                xm = jnp.concatenate([xh, zero] if own == 0 else [zero, xh], axis=0)
                lrow, drow = logs_s[h, :], delta_s[h, :]
                sums = None
                grads = None
                for t0, width in ((128, 256), (0, 128)):
                    t = slice(t0, t0 + 128)
                    gap = lcol[i, t, j:j + 1] - lrow[:, :width] + mask[t, :width]
                    decay = jnp.exp(gap)
                    dm = jnp.dot(g_in[t, cols], xm[:, :width], preferred_element_type=f32)
                    pulled = dm * decay * drow[:, :width]
                    dscore[t, :width] += pulled
                    sc = score[t, :width]
                    e = pulled * sc
                    rcol[i, t, j:j + 1] = jnp.sum(e, axis=1, keepdims=True)
                    es = jnp.sum(e, axis=0, keepdims=True)
                    mixed = jnp.dot(
                        GT[r, t], (sc * decay).astype(bf16), preferred_element_type=f32
                    )
                    if t0:
                        sums, grads = es, mixed
                        Y[r, 128:] = mixed[:, 128:]
                    else:
                        csum[h, :] = jnp.concatenate([sums[:, :128] + es, sums[:, 128:]], axis=1)
                        Y[r, :128] = grads[:, :128] + mixed

    def forward(way, i):
        for j in range(HPC):
            r = rows_at(i * CR + j * 64, 64)
            h = pl.ds(HPC * i + j, 1)
            FB[way, r, :] = (
                FB[way, r, :].astype(f32) + keep_s[h, :] * zin[way, r, :].astype(f32)
            ).astype(bf16)
        send(way, i).start()

    def state_terms(way, i):
        rc = rows_at(i * CR, CR)
        state = zin[way, rc, :]
        UV[way, rc, :] = lax.dot_general(
            state, vec[way], (((1,), (1,)), ((), ())), preferred_element_type=f32
        )
        dvec[way] += lax.dot_general(
            A[way, rc, :], state, (((0,), (0,)), ((), ())), preferred_element_type=f32
        )

    def finish(i):
        for pair in range(HPC // 2):
            for own in range(2):
                j = pair * 2 + own
                r = rows_at(i * CR + j * 64, 64)
                h = pl.ds(HPC * i + j, 1)
                v = UV[1, r, :]
                xt = XT[r, :].astype(f32)
                yt = Y[r, :] + tail_s[h, :] * v
                qsum[h, :] = jnp.sum(xt * yt, axis=0, keepdims=True)
                xvsum[h, :] = jnp.sum(xt * v, axis=0, keepdims=True)
                gusum[h, :] = jnp.sum(GT[r, :].astype(f32) * UV[0, r, :], axis=0, keepdims=True)
                lsum[h, :] = jnp.sum(
                    zin[0, r, :].astype(f32) * zin[1, r, :].astype(f32), axis=0, keepdims=True
                )
                Y[r, :] = delta_s[h, :] * yt
            rp = rows_at(i * CR + pair * 128, 128)
            dx[:, columns(i * CR + pair * 128, 128)] = Y[rp, :].astype(bf16).T

    def step(k, _):
        @pl.when(k < CH)
        def _():
            local(k)

            @pl.when(inner)
            def _():
                send(near, k).wait_recv()
                forward(near, k)
                state_terms(near, k)

        @pl.when(k >= LAG)
        def _():
            i = k - LAG
            send(far, i).wait_recv()

            @pl.when(inner)
            def _():
                forward(far, i)

            state_terms(far, i)
            finish(i)

        return 0

    lax.fori_loop(0, CH + LAG, step, 0)
    dx_copy = pltpu.make_async_copy(dx, dx_out, dx_sem)
    dx_copy.start()

    rows = jnp.concatenate([rcol[i] for i in range(CH)], axis=1).T
    pulls = td_s[...] * xvsum[...]
    change = rows - csum[...] + head_s[...] * gusum[...] - pulls
    at_end = jnp.sum(pulls + keep_s[...] * lsum[...], axis=1, keepdims=True)
    tok_row = lax.broadcasted_iota(jnp.int32, (32, TOK), 1)
    change = change + jnp.where(tok_row == TOK - 1, at_end, 0.0)
    t_at = lax.broadcasted_iota(jnp.int32, (TOK, TOK), 0)
    s_at = lax.broadcasted_iota(jnp.int32, (TOK, TOK), 1)
    down_to = jnp.where(t_at >= s_at, 1.0, 0.0).astype(f32)
    dlog = jnp.dot(change, down_to, precision=highest, preferred_element_type=f32)
    ddelta = qsum[...] - rate[...] * dlog
    raw_t = raw[...].T
    valid_row = jnp.where(tok_row < count, 1.0, 0.0).astype(f32)
    raw_grad = ddelta * valid_row * (1.0 / (1.0 + jnp.exp(-raw_t)))
    rate_grad = jnp.sum(-delta_s[...] * dlog, axis=1, keepdims=True)
    bias_grad = jnp.sum(raw_grad, axis=1, keepdims=True)
    lane = lax.broadcasted_iota(jnp.int32, (32, 128), 1)
    small[...] = jnp.where(
        lane == 0, rate_grad, jnp.where(lane == 1, bias_grad, count.astype(f32))
    )
    ds = dscore[...].astype(bf16)
    WRX[x, c, :, 0:N] = (
        dvec[1]
        + lax.dot_general(ds, vec[0], (((0,), (0,)), ((), ())), preferred_element_type=f32)
    ).astype(bf16)
    WRX[x, c, :, N:2 * N] = (
        dvec[0] + jnp.dot(ds, vec[1], preferred_element_type=f32)
    ).astype(bf16)
    WRX[x, c, :, 2 * N:] = raw_grad.T.astype(bf16)

    def wr_to(group, device, send_index, recv_index):
        return remote(
            WRX.at[group, c], WRX.at[group, c], wxsend.at[send_index], wxrecv.at[recv_index], device
        )

    own_wr = go(wr_to(x, sibling, 0, 0))
    for s in (1, 3, 2):
        go(wr_to(x, shifted(z, c, y, x, dx=s), s, s))
    s_copy = go(remote(small, sib_small, csend.at[0], crecv.at[0], sibling))
    own_wr.wait_recv()

    def product(m):
        index = slot((m // 4, m % 4))
        value = lax.dot_general(
            WRX[x, 0], H[0, :, columns(index * 256, 256)], (((0,), (0,)), ((), ())),
            preferred_element_type=f32,
        )
        value += lax.dot_general(
            WRX[x, 1], H[1, :, columns(index * 256, 256)], (((0,), (0,)), ((), ())),
            preferred_element_type=f32,
        )
        sendbuf[m] = value.astype(bf16)

    def reduced(half, src, m, device):
        return remote(
            sendbuf.at[src, half_rows(half)], rbuf.at[half, m],
            gsend.at[half, m], grecv.at[half, m], device,
        )

    def up(half, m):
        ez, ey = origin(half, (m // 4, m % 4))
        go(reduced(half, m, m, shifted(z, c, y, x, dz=ez, dy=ey)))

    def total(half, m):
        value = sendbuf[m, row_half(half)].astype(f32)
        for _, name in children(half, (m // 4, m % 4)):
            k = name[0] * 4 + name[1]
            reduced(half, m, k, sibling).wait_recv()
            value = value + rbuf[half, k].astype(f32)
        return value

    done = set()
    climb = []
    for half, m in reversed(ORDER):
        if m not in done:
            product(m)
            done.add(m)
        if children(half, (m // 4, m % 4)):
            climb.append((half, m))
        else:
            up(half, m)
    product(0)

    s_copy.wait_recv()
    y_small[y] = small[...] + sib_small[...]
    for s in (1, 2, 3):
        go(remote(
            y_small.at[y], y_small.at[y], csend.at[s], crecv.at[s], shifted(z, c, y, x, dy=s)
        ))

    def small_z():
        for s in (1, 2, 3):
            remote(
                y_small.at[y], y_small.at[(y - s + 4) % 4], csend.at[s], crecv.at[s], sibling
            ).wait_recv()
        z_small[z] = (y_small[0] + y_small[1]) + (y_small[2] + y_small[3])
        for s in (1, 2, 3):
            go(remote(
                z_small.at[z], z_small.at[z], csend.at[3 + s], crecv.at[3 + s],
                shifted(z, c, y, x, dz=s),
            ))

    def small_end():
        for s in (1, 2, 3):
            remote(
                z_small.at[z], z_small.at[(z - s + 4) % 4], csend.at[3 + s], crecv.at[3 + s], sibling
            ).wait_recv()
        small_out[...] = (z_small[0] + z_small[1]) + (z_small[2] + z_small[3])

    def tile(r, k):
        return pl.ds((r * 4 + k) * 256, 256)

    def hidden_own():
        for r in range(2):
            for k in range(4):
                Y[tile(r, k), :] = jnp.dot(WRX[x, r], W[x * 4 + k], preferred_element_type=f32)

    def pass_on(s):
        group = (x - s + 4) % 4
        remote(
            WRX.at[group, c], WRX.at[group, c], wxsend.at[s], wxrecv.at[s], sibling
        ).wait_recv()
        go(remote(WRX.at[group, c], WRX.at[group, c], fsend.at[s], frecv.at[s], sibling))

    def hidden_add(s):
        group = (x - s + 4) % 4
        remote(
            WRX.at[group, other], WRX.at[group, other], fsend.at[s], frecv.at[s], sibling
        ).wait_recv()
        for k in range(4):
            remote(
                W.at[0], WX.at[group, k], xsend.at[0], xrecv.at[group, k], sibling
            ).wait_recv()
        for r in range(2):
            for k in range(4):
                Y[tile(r, k), :] += jnp.dot(
                    WRX[group, r], WX[group, k], preferred_element_type=f32
                )

    def hidden_end():
        for r in range(2):
            for k in range(4):
                XT[tile(r, k), :] = Y[tile(r, k), :].astype(bf16)
        for k in range(4):
            go(remote(
                XT.at[pl.ds((other * 4 + k) * 256, 256)],
                hid_out.at[:, columns(c * 1024 + k * 256, 256)],
                rsend.at[k], rrecv.at[k], sibling,
            ))
        for k in range(4):
            hid_out[:, columns(c * 1024 + k * 256, 256)] = XT[rows_at((c * 4 + k) * 256, 256), :]

    beside = [
        hidden_own, small_z, lambda: pass_on(1), lambda: pass_on(3), lambda: hidden_add(1),
        lambda: hidden_add(3), lambda: pass_on(2), small_end, lambda: hidden_add(2), hidden_end,
    ]
    for half, m in climb:
        sendbuf[m, row_half(half)] = total(half, m).astype(bf16)
        up(half, m)
        if beside:
            beside.pop(0)()
    for work in beside:
        work()
    sums = small_out[...]
    small_out[...] = sums / sums[:, 2:3]
    tokens = sums[0:1, 2:3]
    for copy in m_loads:
        copy.wait()
    first = adam_direction(total(0, 0) / tokens, mom[row_half(0)], sec[row_half(0)])
    pu_out[0:CUT] = first
    second = adam_direction(total(1, 0) / tokens, mom[row_half(1)], sec[row_half(1)])
    pu_out[CUT:512] = second[:512 - CUT]
    du_out[...] = second[512 - CUT:]
    for k in range(4):
        remote(
            XT.at[pl.ds(k * 256, 256)], hid_out.at[:, columns(other * 1024 + k * 256, 256)],
            rsend.at[k], rrecv.at[k], sibling,
        ).wait_recv()

    for copy in started:
        copy.wait_send()
    for k in range(16):
        @pl.when(k // 4 != x)
        def _():
            across(k, x, k // 4).wait_send()

    def drain(i, _):
        send(near, i).wait_send()

        @pl.when(inner)
        def _():
            send(far, i).wait_send()

        return 0

    lax.fori_loop(0, CH, drain, 0)
    dx_copy.wait()


VM = pl.BlockSpec(memory_space=pltpu.VMEM)
ANY = pl.BlockSpec(memory_space=pl.ANY)
SM = pl.BlockSpec(memory_space=pltpu.SMEM)
DMA = pltpu.SemaphoreType.DMA


def shards(
    hidden,
    inputs,
    upstream,
    proj_weight,
    delta_weight,
    decay_rate,
    step_bias,
    proj_moment,
    proj_second,
    delta_moment,
    delta_second,
    doc_lengths,
    valid_counts,
):
    def vmem(shape, dtype=f32):
        return pltpu.VMEM(shape, dtype)

    row = vmem((32, TOK))
    input_grad, hidden_grad, proj_update, delta_update, sums = pl.pallas_call(
        layer_kernel,
        out_shape=(
            jax.ShapeDtypeStruct((TOK, 2048), bf16),
            jax.ShapeDtypeStruct((TOK, 2048), bf16),
            jax.ShapeDtypeStruct((512, 256), f32),
            jax.ShapeDtypeStruct((32, 256), f32),
            jax.ShapeDtypeStruct((32, 128), f32),
        ),
        in_specs=[ANY, ANY, ANY, ANY, ANY, VM, VM, ANY, ANY, ANY, ANY, SM, SM],
        out_specs=(ANY, VM, VM, VM, VM),
        scratch_shapes=[
            vmem((16, ROWS, 256), bf16),
            vmem((2, TOK, D // 2), bf16),
            vmem((4, 4, ROWS, 256), bf16),
            vmem((2, TOK, ROWS)),
            vmem((TOK, ROWS)),
            vmem((TOK, 512), bf16),
            vmem((TOK, 32)),
            vmem((TOK, 2048), bf16),
            vmem((TOK, 2048), bf16),
            vmem((ROWS, 256)),
            vmem((ROWS, 256)),
            vmem((2048, TOK), bf16),
            vmem((2048, TOK), bf16),
            vmem((2, 2048, TOK), bf16),
            vmem((2, 2048, N), bf16),
            vmem((2, 2048, N), bf16),
            vmem((2, 2048, TOK)),
            vmem((2048, TOK)),
            vmem((TOK, 2048), bf16),
            vmem((TOK, TOK)),
            vmem((TOK, TOK)),
            vmem((TOK, TOK)),
            vmem((2, TOK, N)),
            vmem((2, TOK, N), bf16),
            row, row, row, row, row, row,
            vmem((CH, TOK, HPC)),
            vmem((CH, TOK, HPC)),
            row, row, row, row, row,
            vmem((4, 2, TOK, ROWS), bf16),
            vmem((16, ROWS, 256), bf16),
            vmem((2, 16, CUT, 256), bf16),
            vmem((32, 128)), vmem((32, 128)), vmem((4, 32, 128)), vmem((4, 32, 128)),
            DMA((2,)), DMA((4,)), DMA((4,)), DMA((4,)), DMA((2, 16)), DMA((2, 16)), DMA, DMA,
            DMA((16,)), DMA((4, 4)), DMA((2,)), DMA((4,)),
            DMA((2, CH)), DMA((2, CH)), DMA, DMA((4,)), DMA((4,)), DMA((4,)), DMA((4,)),
            DMA((2, 16)), DMA((2, 16)), DMA((4,)), DMA((4,)), DMA((7,)), DMA((7,)),
        ],
        compiler_params=pltpu.CompilerParams(
            collective_id=0, has_side_effects=True, vmem_limit_bytes=60 * 2**20
        ),
        name="layer_backward",
    )(
        hidden, inputs, upstream, proj_weight, delta_weight, decay_rate.reshape(32, 1),
        step_bias.reshape(1, 32), proj_moment, proj_second, delta_moment, delta_second,
        doc_lengths, valid_counts,
    )
    return (
        input_grad[None], hidden_grad[None], sums[:, 0], sums[:, 1], proj_update, delta_update
    )


def solution(mesh):
    return jax.shard_map(
        shards,
        mesh=mesh,
        in_specs=(
            P("dp", "context", None),
            P("dp", "context", "tensor"),
            P("dp", "context", "tensor"),
            P("tensor", ("dp", "context")),
            P("tensor", ("dp", "context")),
            P("tensor"),
            P("tensor"),
            P("tensor", ("dp", "context")),
            P("tensor", ("dp", "context")),
            P("tensor", ("dp", "context")),
            P("tensor", ("dp", "context")),
            P("dp", None),
            P("dp", "context"),
        ),
        out_specs=(
            P("dp", "context", "tensor"),
            P("dp", "context", "tensor"),
            P("tensor"),
            P("tensor"),
            P("tensor", ("dp", "context")),
            P("tensor", ("dp", "context")),
        ),
        check_vma=False,
    )
```

```python
import jax
import jax.numpy as jnp
from jax import lax
from jax.experimental import pallas as pl
from jax.experimental.pallas import tpu as pltpu
from jax.sharding import PartitionSpec as P

N = 256
D = 8192
TOK = 256
ROWS = 544
CUT = 272
ORDER = (
    (1, 4), (0, 1), (0, 3), (1, 12), (0, 4), (1, 1),
    (1, 3), (0, 12), (0, 5), (1, 5), (1, 7), (0, 13),
    (0, 7), (0, 2), (1, 15), (0, 15), (0, 8), (1, 13),
    (1, 8), (1, 14), (0, 9), (1, 2), (0, 14), (1, 11),
    (0, 6), (1, 6), (0, 11), (1, 10), (1, 9), (0, 10),
)
MESH = pl.DeviceIdType.MESH
f32 = jnp.float32
bf16 = jnp.bfloat16

beta_one = 0.9
beta_two = 0.95
adam_eps = 1e-08
adam_step = 100
highest = lax.Precision.HIGHEST

HPC = 2
LAG = 4
CH = 32 // HPC
CR = HPC * 64
PIECES = [(i, j) for i in range(4) for j in range(4)]


def origin(half, piece):
    sz, sy = piece
    if half == 0:
        if sz == 0:
            return (0, 1) if sy in (1, 2) else (0, -1)
        if sz == 2:
            return (1, 0) if sy in (0, 1) else (-1, 0)
        return (1, 0) if sz == 1 else (-1, 0)
    if sy == 0:
        return (1, 0) if sz == 1 else (-1, 0)
    if sy == 2:
        return (0, 1) if sz in (0, 1) else (0, -1)
    return (0, 1) if sy == 1 else (0, -1)


def children(half, piece):
    found = []
    for other in PIECES:
        if other == (0, 0):
            continue
        ez, ey = origin(half, other)
        if ((other[0] - ez) % 4, (other[1] - ey) % 4) == piece:
            found.append(((-ez, -ey), other))
    return found


def place():
    dp, y, x = lax.axis_index("dp"), lax.axis_index("context"), lax.axis_index("tensor")
    return dp // 2, dp % 2, y, x


def shifted(z, c, y, x, dz=0, dy=0, dx=0):
    return (((z + dz + 4) % 4) * 2 + c, (y + dy + 4) % 4, (x + dx + 4) % 4)


def greet(devices):
    barrier = pltpu.get_barrier_semaphore()
    for device in devices:
        pl.semaphore_signal(barrier, inc=1, device_id=device, device_id_type=MESH)
    pl.semaphore_wait(barrier, len(devices))


def half_rows(half):
    return pl.ds(half * CUT, CUT)


def columns(start, size):
    return pl.ds(pl.multiple_of(start, size), size)


def row_half(half):
    return slice(half * CUT, (half + 1) * CUT)


def rows_at(start, size):
    return pl.ds(pl.multiple_of(start, size), size)


def adam_direction(grad, moment, second):
    moment = beta_one * moment + (1.0 - beta_one) * grad
    second = beta_two * second + (1.0 - beta_two) * grad * grad
    corrected = moment / (1.0 - beta_one**adam_step)
    return corrected / (jnp.sqrt(second / (1.0 - beta_two**adam_step)) + adam_eps)


def layer_kernel(
    hidden, inputs, upstream, pw, dw, rate, step_bias, pm, ps, dmo, dse, docs, counts,
    dx_out, hid_out, pu_out, du_out, small_out,
    W, H, WX, acc, part, projected, raw, x_in, g_in, mom, sec,
    XT, GT, A, FB, zin, UV, Y, dx, mask, score, dscore, dvec, vec,
    delta_s, tail_s, head_s, logs_s, keep_s, td_s, lcol, rcol, csum, qsum, xvsum, gusum, lsum,
    rate_s, WRX, sendbuf, rbuf, small, sib_small, y_small, z_small,
    load_sem, hload_sem, hsend, hrecv, wsend, wrecv, psend, precv, xsend, xrecv, in_sem, m_sem,
    ssem, rsem, dx_sem, wxsend, wxrecv, fsend, frecv, gsend, grecv, rsend, rrecv, csend, crecv,
):
    z, c, y, x = place()
    other = 1 - c
    sibling = (z * 2 + other, y, x)

    def remote(src, dst, send_sem, recv_sem, device):
        return pltpu.make_async_remote_copy(
            src_ref=src, dst_ref=dst, send_sem=send_sem, recv_sem=recv_sem,
            device_id=device, device_id_type=MESH,
        )

    started = []

    def go(copy):
        copy.start()
        started.append(copy)
        return copy

    def slot(piece):
        return ((z + piece[0]) % 4) * 4 + (y + piece[1]) % 4

    mine = slot((0, 0))
    loads = [
        pltpu.make_async_copy(pw, W.at[mine, pl.ds(0, 512)], load_sem.at[0]),
        pltpu.make_async_copy(dw, W.at[mine, pl.ds(512, 32)], load_sem.at[1]),
    ]
    hloads = [
        pltpu.make_async_copy(
            hidden.at[0, :, columns((2 * k + c) * 1024, 1024)],
            H.at[c, :, pl.ds(k * 1024, 1024)],
            hload_sem.at[k],
        )
        for k in range(4)
    ]
    in_loads = [
        pltpu.make_async_copy(inputs.at[0], x_in, in_sem.at[0]),
        pltpu.make_async_copy(upstream.at[0], g_in, in_sem.at[1]),
    ]
    m_loads = [
        pltpu.make_async_copy(pm, mom.at[pl.ds(0, 512)], m_sem.at[0]),
        pltpu.make_async_copy(dmo, mom.at[pl.ds(512, 32)], m_sem.at[1]),
        pltpu.make_async_copy(ps, sec.at[pl.ds(0, 512)], m_sem.at[2]),
        pltpu.make_async_copy(dse, sec.at[pl.ds(512, 32)], m_sem.at[3]),
    ]
    for copy in loads + hloads + in_loads + m_loads:
        copy.start()
    greet(
        [sibling]
        + [shifted(z, c, y, x, dz=s) for s in (1, 2, 3)]
        + [shifted(z, c, y, x, dy=s) for s in (1, 2, 3)]
        + [shifted(z, c, y, x, dx=s) for s in (1, 2, 3)]
    )
    for copy in loads:
        copy.wait()

    def gathered(half, index, name, device):
        part_ref = W.at[index, half_rows(half)]
        m = name[0] * 4 + name[1]
        return remote(part_ref, part_ref, wsend.at[half, m], wrecv.at[half, m], device)

    def relay(half, piece, axis=None):
        for (ez, ey), name in children(half, piece):
            if axis is None or (axis == 0) == (ez != 0):
                go(gathered(half, slot(piece), name, shifted(z, c, y, x, dz=ez, dy=ey)))

    def across(index, source, group):
        return remote(
            W.at[index], WX.at[source, index % 4],
            xsend.at[index], xrecv.at[source, index % 4], (z * 2 + c, y, group),
        )

    def complete(piece):
        index = slot(piece)
        group = (z + piece[0]) % 4

        @pl.when(group != x)
        def _():
            across(index, x, group).start()

    def multiply(piece):
        index = slot(piece)
        for r in range(2):
            acc[r] += lax.dot_general(
                H[r, :, columns(index * 256, 256)], W[index],
                (((1,), (1,)), ((), ())), preferred_element_type=f32,
            )

    relay(0, (0, 0), 1)
    relay(1, (0, 0), 0)
    relay(0, (0, 0), 0)
    relay(1, (0, 0), 1)
    hremote = []
    for k in range(4):
        hremote.append(go(remote(
            hidden.at[0, :, columns((2 * k + other) * 1024, 1024)],
            H.at[c, :, pl.ds(k * 1024, 1024)], hsend.at[k], hrecv.at[k], sibling,
        )))
    complete((0, 0))
    acc[...] = jnp.zeros_like(acc)
    for copy in in_loads:
        copy.wait()

    base = y * TOK
    count = counts[0, 0]
    starts = []
    at = jnp.int32(0)
    for k in range(4):
        starts.append(at)
        at = at + docs[0, k]

    def marks(position):
        total = jnp.zeros(position.shape, jnp.int32)
        for s in starts:
            total = total + jnp.where((s >= base) & (position >= s - base), 1, 0)
        return total

    tok_row = lax.broadcasted_iota(jnp.int32, (32, TOK), 1)
    t_at = lax.broadcasted_iota(jnp.int32, (TOK, TOK), 0)
    s_at = lax.broadcasted_iota(jnp.int32, (TOK, TOK), 1)
    inside = (t_at >= s_at) & (marks(t_at) == marks(s_at)) & (t_at < count)
    mask[...] = jnp.where(inside, 0.0, -1e30).astype(f32)

    def turn(p, _):
        cols = columns(p * 128, 128)
        XT[rows_at(p * 128, 128), :] = x_in[:, cols].T
        GT[rows_at(p * 128, 128), :] = g_in[:, cols].T
        return 0

    lax.fori_loop(0, 16, turn, 0)
    dvec[...] = jnp.zeros_like(dvec)
    dscore[...] = jnp.zeros_like(dscore)
    near = y // 2
    far = 1 - near
    inner = (y == 1) | (y == 2)

    @pl.when(jnp.logical_not(inner))
    def _():
        zin[near] = jnp.zeros((2048, N), bf16)
        UV[near] = jnp.zeros((2048, TOK), f32)

    seen = {}
    ready = False
    for half, m in ORDER:
        piece = (m // 4, m % 4)
        gathered(half, slot(piece), piece, sibling).wait_recv()
        relay(half, piece)
        seen[m] = seen.get(m, 0) + 1
        if seen[m] == 2:
            complete(piece)
            if not ready:
                for copy in hloads:
                    copy.wait()
                for copy in hremote:
                    copy.wait_recv()
                multiply((0, 0))
                ready = True
            multiply(piece)
    exchange = go(remote(acc.at[other], part, psend, precv, sibling))
    exchange.wait_recv()
    total_acc = acc[c] + part[...]
    projected[...] = total_acc[:, :512].astype(bf16)
    raw[...] = total_acc[:, 512:] + step_bias[...]

    def onward(way):
        return shifted(z, c, y, x, dy=1 - 2 * way)

    marks_row = marks(tok_row)
    marks_last = marks(jnp.full((32, TOK), TOK - 1, jnp.int32))
    valid_row = jnp.where(tok_row < count, 1.0, 0.0).astype(f32)
    up_to = jnp.where(t_at <= s_at, 1.0, 0.0).astype(f32)
    raw_t = raw[...].T
    rate_s[...] = jnp.broadcast_to(rate[...], (128, 32)).T
    rate_col = rate_s[:, 0:1]
    delta = valid_row * (jnp.maximum(raw_t, 0.0) + jnp.log1p(jnp.exp(-jnp.abs(raw_t))))
    logs = jnp.dot(-rate_col * delta, up_to, precision=highest, preferred_element_type=f32)
    last = logs[:, TOK - 1:TOK]
    tail = jnp.where(marks_row == marks_last, jnp.exp(last - logs), 0.0)
    head = jnp.where(marks_row == 0, jnp.exp(logs), 0.0) * valid_row
    keep = jnp.where(marks_last == 0, jnp.exp(jnp.broadcast_to(last, (32, TOK))), 0.0)
    delta_s[...] = delta
    tail_s[...] = tail
    head_s[...] = head
    logs_s[...] = logs
    keep_s[...] = keep
    td_s[...] = tail * delta
    writes, reads = projected[:, 0:N], projected[:, N:2 * N]
    vec[0] = reads
    vec[1] = writes

    def send(way, i):
        return remote(
            FB.at[way, rows_at(i * CR, CR)], zin.at[way, rows_at(i * CR, CR)],
            ssem.at[way, i], rsem.at[way, i], onward(way),
        )

    def ends(i, _):
        for j in range(HPC):
            r = rows_at(i * CR + j * 64, 64)
            h = pl.ds(HPC * i + j, 1)
            A[0, r, :] = (GT[r, :].astype(f32) * head_s[h, :]).astype(bf16)
            A[1, r, :] = (XT[r, :].astype(f32) * td_s[h, :]).astype(bf16)
        rc = rows_at(i * CR, CR)
        FB[0, rc, :] = jnp.dot(A[1, rc, :], writes, preferred_element_type=f32).astype(bf16)
        FB[1, rc, :] = jnp.dot(A[0, rc, :], reads, preferred_element_type=f32).astype(bf16)

        @pl.when(jnp.logical_not(inner))
        def _():
            send(near, i).start()

        return 0

    lax.fori_loop(0, CH, ends, 0)
    logs_col = logs.T
    for i in range(CH):
        lcol[i] = logs_col[:, HPC * i:HPC * i + HPC]
    score[...] = lax.dot_general(
        reads, writes, (((1,), (1,)), ((), ())), preferred_element_type=f32
    )

    def local(i):
        for pair in range(HPC // 2):
            cols = columns(i * CR + pair * 128, 128)
            zero = jnp.zeros((64, TOK), bf16)
            for own in range(2):
                j = pair * 2 + own
                r = rows_at(i * CR + j * 64, 64)
                h = pl.ds(HPC * i + j, 1)
                xh = XT[r, :]
                xm = jnp.concatenate([xh, zero] if own == 0 else [zero, xh], axis=0)
                lrow, drow = logs_s[h, :], delta_s[h, :]
                sums = None
                grads = None
                for t0, width in ((128, 256), (0, 128)):
                    t = slice(t0, t0 + 128)
                    gap = lcol[i, t, j:j + 1] - lrow[:, :width] + mask[t, :width]
                    decay = jnp.exp(gap)
                    dm = jnp.dot(g_in[t, cols], xm[:, :width], preferred_element_type=f32)
                    pulled = dm * decay * drow[:, :width]
                    dscore[t, :width] += pulled
                    sc = score[t, :width]
                    e = pulled * sc
                    rcol[i, t, j:j + 1] = jnp.sum(e, axis=1, keepdims=True)
                    es = jnp.sum(e, axis=0, keepdims=True)
                    mixed = jnp.dot(
                        GT[r, t], (sc * decay).astype(bf16), preferred_element_type=f32
                    )
                    if t0:
                        sums, grads = es, mixed
                        Y[r, 128:] = mixed[:, 128:]
                    else:
                        csum[h, :] = jnp.concatenate([sums[:, :128] + es, sums[:, 128:]], axis=1)
                        Y[r, :128] = grads[:, :128] + mixed

    def forward(way, i):
        for j in range(HPC):
            r = rows_at(i * CR + j * 64, 64)
            h = pl.ds(HPC * i + j, 1)
            FB[way, r, :] = (
                FB[way, r, :].astype(f32) + keep_s[h, :] * zin[way, r, :].astype(f32)
            ).astype(bf16)
        send(way, i).start()

    def state_terms(way, i):
        rc = rows_at(i * CR, CR)
        state = zin[way, rc, :]
        UV[way, rc, :] = lax.dot_general(
            state, vec[way], (((1,), (1,)), ((), ())), preferred_element_type=f32
        )
        dvec[way] += lax.dot_general(
            A[way, rc, :], state, (((0,), (0,)), ((), ())), preferred_element_type=f32
        )

    def finish(i):
        for pair in range(HPC // 2):
            for own in range(2):
                j = pair * 2 + own
                r = rows_at(i * CR + j * 64, 64)
                h = pl.ds(HPC * i + j, 1)
                v = UV[1, r, :]
                xt = XT[r, :].astype(f32)
                yt = Y[r, :] + tail_s[h, :] * v
                qsum[h, :] = jnp.sum(xt * yt, axis=0, keepdims=True)
                xvsum[h, :] = jnp.sum(xt * v, axis=0, keepdims=True)
                gusum[h, :] = jnp.sum(GT[r, :].astype(f32) * UV[0, r, :], axis=0, keepdims=True)
                lsum[h, :] = jnp.sum(
                    zin[0, r, :].astype(f32) * zin[1, r, :].astype(f32), axis=0, keepdims=True
                )
                Y[r, :] = delta_s[h, :] * yt
            rp = rows_at(i * CR + pair * 128, 128)
            dx[:, columns(i * CR + pair * 128, 128)] = Y[rp, :].astype(bf16).T

    def step(k, _):
        @pl.when(k < CH)
        def _():
            local(k)

            @pl.when(inner)
            def _():
                send(near, k).wait_recv()
                forward(near, k)
                state_terms(near, k)

        @pl.when(k >= LAG)
        def _():
            i = k - LAG
            send(far, i).wait_recv()

            @pl.when(inner)
            def _():
                forward(far, i)

            state_terms(far, i)
            finish(i)

        return 0

    lax.fori_loop(0, CH + LAG, step, 0)
    dx_copy = pltpu.make_async_copy(dx, dx_out, dx_sem)
    dx_copy.start()

    rows = jnp.concatenate([rcol[i] for i in range(CH)], axis=1).T
    pulls = td_s[...] * xvsum[...]
    change = rows - csum[...] + head_s[...] * gusum[...] - pulls
    at_end = jnp.sum(pulls + keep_s[...] * lsum[...], axis=1, keepdims=True)
    tok_row = lax.broadcasted_iota(jnp.int32, (32, TOK), 1)
    change = change + jnp.where(tok_row == TOK - 1, at_end, 0.0)
    t_at = lax.broadcasted_iota(jnp.int32, (TOK, TOK), 0)
    s_at = lax.broadcasted_iota(jnp.int32, (TOK, TOK), 1)
    down_to = jnp.where(t_at >= s_at, 1.0, 0.0).astype(f32)
    dlog = jnp.dot(change, down_to, precision=highest, preferred_element_type=f32)
    ddelta = qsum[...] - rate_s[:, 0:1] * dlog
    raw_t = raw[...].T
    valid_row = jnp.where(tok_row < count, 1.0, 0.0).astype(f32)
    raw_grad = ddelta * valid_row * (1.0 / (1.0 + jnp.exp(-raw_t)))
    rate_grad = jnp.sum(-delta_s[...] * dlog, axis=1, keepdims=True)
    bias_grad = jnp.sum(raw_grad, axis=1, keepdims=True)
    lane = lax.broadcasted_iota(jnp.int32, (32, 128), 1)
    small[...] = jnp.where(
        lane == 0, rate_grad, jnp.where(lane == 1, bias_grad, count.astype(f32))
    )
    ds = dscore[...].astype(bf16)
    WRX[x, c, :, 0:N] = (
        dvec[1]
        + lax.dot_general(ds, vec[0], (((0,), (0,)), ((), ())), preferred_element_type=f32)
    ).astype(bf16)
    WRX[x, c, :, N:2 * N] = (
        dvec[0] + jnp.dot(ds, vec[1], preferred_element_type=f32)
    ).astype(bf16)
    WRX[x, c, :, 2 * N:] = raw_grad.T.astype(bf16)

    def wr_to(group, device, send_index, recv_index):
        return remote(
            WRX.at[group, c], WRX.at[group, c], wxsend.at[send_index], wxrecv.at[recv_index], device
        )

    own_wr = go(wr_to(x, sibling, 0, 0))
    for s in (1, 3, 2):
        go(wr_to(x, shifted(z, c, y, x, dx=s), s, s))
    s_copy = go(remote(small, sib_small, csend.at[0], crecv.at[0], sibling))
    own_wr.wait_recv()

    def product(m):
        index = slot((m // 4, m % 4))
        value = lax.dot_general(
            WRX[x, 0], H[0, :, columns(index * 256, 256)], (((0,), (0,)), ((), ())),
            preferred_element_type=f32,
        )
        value += lax.dot_general(
            WRX[x, 1], H[1, :, columns(index * 256, 256)], (((0,), (0,)), ((), ())),
            preferred_element_type=f32,
        )
        sendbuf[m] = value.astype(bf16)

    def reduced(half, src, m, device):
        return remote(
            sendbuf.at[src, half_rows(half)], rbuf.at[half, m],
            gsend.at[half, m], grecv.at[half, m], device,
        )

    def up(half, m):
        ez, ey = origin(half, (m // 4, m % 4))
        go(reduced(half, m, m, shifted(z, c, y, x, dz=ez, dy=ey)))

    def total(half, m):
        value = sendbuf[m, row_half(half)].astype(f32)
        for _, name in children(half, (m // 4, m % 4)):
            k = name[0] * 4 + name[1]
            reduced(half, m, k, sibling).wait_recv()
            value = value + rbuf[half, k].astype(f32)
        return value

    done = set()
    climb = []
    for half, m in reversed(ORDER):
        if m not in done:
            product(m)
            done.add(m)
        if children(half, (m // 4, m % 4)):
            climb.append((half, m))
        else:
            up(half, m)
    product(0)

    s_copy.wait_recv()
    y_small[y] = small[...] + sib_small[...]
    for s in (1, 2, 3):
        go(remote(
            y_small.at[y], y_small.at[y], csend.at[s], crecv.at[s], shifted(z, c, y, x, dy=s)
        ))

    def small_z():
        for s in (1, 2, 3):
            remote(
                y_small.at[y], y_small.at[(y - s + 4) % 4], csend.at[s], crecv.at[s], sibling
            ).wait_recv()
        z_small[z] = (y_small[0] + y_small[1]) + (y_small[2] + y_small[3])
        for s in (1, 2, 3):
            go(remote(
                z_small.at[z], z_small.at[z], csend.at[3 + s], crecv.at[3 + s],
                shifted(z, c, y, x, dz=s),
            ))

    def small_end():
        for s in (1, 2, 3):
            remote(
                z_small.at[z], z_small.at[(z - s + 4) % 4], csend.at[3 + s], crecv.at[3 + s], sibling
            ).wait_recv()
        small_out[...] = (z_small[0] + z_small[1]) + (z_small[2] + z_small[3])

    def tile(r, k):
        return pl.ds((r * 4 + k) * 256, 256)

    def hidden_own():
        for r in range(2):
            for k in range(4):
                Y[tile(r, k), :] = jnp.dot(WRX[x, r], W[x * 4 + k], preferred_element_type=f32)

    def pass_on(s):
        group = (x - s + 4) % 4
        remote(
            WRX.at[group, c], WRX.at[group, c], wxsend.at[s], wxrecv.at[s], sibling
        ).wait_recv()
        go(remote(WRX.at[group, c], WRX.at[group, c], fsend.at[s], frecv.at[s], sibling))

    def hidden_add(s):
        group = (x - s + 4) % 4
        remote(
            WRX.at[group, other], WRX.at[group, other], fsend.at[s], frecv.at[s], sibling
        ).wait_recv()
        for k in range(4):
            remote(
                W.at[0], WX.at[group, k], xsend.at[0], xrecv.at[group, k], sibling
            ).wait_recv()
        for r in range(2):
            for k in range(4):
                Y[tile(r, k), :] += jnp.dot(
                    WRX[group, r], WX[group, k], preferred_element_type=f32
                )

    def hidden_end():
        for r in range(2):
            for k in range(4):
                XT[tile(r, k), :] = Y[tile(r, k), :].astype(bf16)
        for k in range(4):
            go(remote(
                XT.at[pl.ds((other * 4 + k) * 256, 256)],
                hid_out.at[:, columns(c * 1024 + k * 256, 256)],
                rsend.at[k], rrecv.at[k], sibling,
            ))
        for k in range(4):
            hid_out[:, columns(c * 1024 + k * 256, 256)] = XT[rows_at((c * 4 + k) * 256, 256), :]

    beside = [
        hidden_own, small_z, lambda: pass_on(1), lambda: pass_on(3), lambda: hidden_add(1),
        lambda: hidden_add(3), lambda: pass_on(2), small_end, lambda: hidden_add(2), hidden_end,
    ]
    for half, m in climb:
        sendbuf[m, row_half(half)] = total(half, m).astype(bf16)
        up(half, m)
        if beside:
            beside.pop(0)()
    for work in beside:
        work()
    sums = small_out[...]
    small_out[...] = sums / sums[:, 2:3]
    tokens = sums[0:1, 2:3]
    for copy in m_loads:
        copy.wait()
    first = adam_direction(total(0, 0) / tokens, mom[row_half(0)], sec[row_half(0)])
    pu_out[0:CUT] = first
    second = adam_direction(total(1, 0) / tokens, mom[row_half(1)], sec[row_half(1)])
    pu_out[CUT:512] = second[:512 - CUT]
    du_out[...] = second[512 - CUT:]
    for k in range(4):
        remote(
            XT.at[pl.ds(k * 256, 256)], hid_out.at[:, columns(other * 1024 + k * 256, 256)],
            rsend.at[k], rrecv.at[k], sibling,
        ).wait_recv()

    for copy in started:
        copy.wait_send()
    for k in range(16):
        @pl.when(k // 4 != x)
        def _():
            across(k, x, k // 4).wait_send()

    def drain(i, _):
        send(near, i).wait_send()

        @pl.when(inner)
        def _():
            send(far, i).wait_send()

        return 0

    lax.fori_loop(0, CH, drain, 0)
    dx_copy.wait()


VM = pl.BlockSpec(memory_space=pltpu.VMEM)
ANY = pl.BlockSpec(memory_space=pl.ANY)
SM = pl.BlockSpec(memory_space=pltpu.SMEM)
DMA = pltpu.SemaphoreType.DMA


def emit_kernel(
    dx, hid, pu, du, sums, dx_out, hid_out, pu_out, du_out, rate_out, bias_out
):
    dx_out[...] = dx[...]
    hid_out[...] = hid[...]
    pu_out[...] = pu[...]
    du_out[...] = du[...]
    turned = sums[...].T
    rate_out[...] = turned[0:1]
    bias_out[...] = turned[1:2]


def shards(
    hidden,
    inputs,
    upstream,
    proj_weight,
    delta_weight,
    decay_rate,
    step_bias,
    proj_moment,
    proj_second,
    delta_moment,
    delta_second,
    doc_lengths,
    valid_counts,
):
    def vmem(shape, dtype=f32):
        return pltpu.VMEM(shape, dtype)

    row = vmem((32, TOK))
    input_grad, hidden_grad, proj_update, delta_update, sums = pl.pallas_call(
        layer_kernel,
        out_shape=(
            jax.ShapeDtypeStruct((TOK, 2048), bf16),
            jax.ShapeDtypeStruct((TOK, 2048), bf16),
            jax.ShapeDtypeStruct((512, 256), f32),
            jax.ShapeDtypeStruct((32, 256), f32),
            jax.ShapeDtypeStruct((32, 128), f32),
        ),
        in_specs=[ANY, ANY, ANY, ANY, ANY, VM, VM, ANY, ANY, ANY, ANY, SM, SM],
        out_specs=(ANY, VM, VM, VM, VM),
        scratch_shapes=[
            vmem((16, ROWS, 256), bf16),
            vmem((2, TOK, D // 2), bf16),
            vmem((4, 4, ROWS, 256), bf16),
            vmem((2, TOK, ROWS)),
            vmem((TOK, ROWS)),
            vmem((TOK, 512), bf16),
            vmem((TOK, 32)),
            vmem((TOK, 2048), bf16),
            vmem((TOK, 2048), bf16),
            vmem((ROWS, 256)),
            vmem((ROWS, 256)),
            vmem((2048, TOK), bf16),
            vmem((2048, TOK), bf16),
            vmem((2, 2048, TOK), bf16),
            vmem((2, 2048, N), bf16),
            vmem((2, 2048, N), bf16),
            vmem((2, 2048, TOK)),
            vmem((2048, TOK)),
            vmem((TOK, 2048), bf16),
            vmem((TOK, TOK)),
            vmem((TOK, TOK)),
            vmem((TOK, TOK)),
            vmem((2, TOK, N)),
            vmem((2, TOK, N), bf16),
            row, row, row, row, row, row,
            vmem((CH, TOK, HPC)),
            vmem((CH, TOK, HPC)),
            row, row, row, row, row,
            vmem((32, 128)),
            vmem((4, 2, TOK, ROWS), bf16),
            vmem((16, ROWS, 256), bf16),
            vmem((2, 16, CUT, 256), bf16),
            vmem((32, 128)), vmem((32, 128)), vmem((4, 32, 128)), vmem((4, 32, 128)),
            DMA((2,)), DMA((4,)), DMA((4,)), DMA((4,)), DMA((2, 16)), DMA((2, 16)), DMA, DMA,
            DMA((16,)), DMA((4, 4)), DMA((2,)), DMA((4,)),
            DMA((2, CH)), DMA((2, CH)), DMA, DMA((4,)), DMA((4,)), DMA((4,)), DMA((4,)),
            DMA((2, 16)), DMA((2, 16)), DMA((4,)), DMA((4,)), DMA((7,)), DMA((7,)),
        ],
        compiler_params=pltpu.CompilerParams(
            collective_id=0, has_side_effects=True, vmem_limit_bytes=60 * 2**20
        ),
        name="layer_backward",
    )(
        hidden, inputs, upstream, proj_weight, delta_weight, decay_rate.reshape(1, 32),
        step_bias.reshape(1, 32), proj_moment, proj_second, delta_moment, delta_second,
        doc_lengths, valid_counts,
    )
    held = (input_grad, hidden_grad, proj_update, delta_update)
    line = jax.ShapeDtypeStruct((1, 32), f32)
    blocks = [pl.BlockSpec((a.shape[0] // 2, a.shape[1]), lambda i: (i, 0)) for a in held]
    input_grad, hidden_grad, proj_update, delta_update, rate_grad, bias_grad = pl.pallas_call(
        emit_kernel,
        out_shape=tuple(jax.ShapeDtypeStruct(a.shape, a.dtype) for a in held) + (line, line),
        grid=(2,),
        in_specs=blocks + [pl.BlockSpec((32, 128), lambda i: (0, 0))],
        out_specs=tuple(blocks) + (pl.BlockSpec((1, 32), lambda i: (0, 0)),) * 2,
        name="emit",
    )(*held, sums)
    return (
        input_grad[None], hidden_grad[None], rate_grad[0], bias_grad[0], proj_update, delta_update
    )


def solution(mesh):
    return jax.shard_map(
        shards,
        mesh=mesh,
        in_specs=(
            P("dp", "context", None),
            P("dp", "context", "tensor"),
            P("dp", "context", "tensor"),
            P("tensor", ("dp", "context")),
            P("tensor", ("dp", "context")),
            P("tensor"),
            P("tensor"),
            P("tensor", ("dp", "context")),
            P("tensor", ("dp", "context")),
            P("tensor", ("dp", "context")),
            P("tensor", ("dp", "context")),
            P("dp", None),
            P("dp", "context"),
        ),
        out_specs=(
            P("dp", "context", "tensor"),
            P("dp", "context", "tensor"),
            P("tensor"),
            P("tensor"),
            P("tensor", ("dp", "context")),
            P("tensor", ("dp", "context")),
        ),
        check_vma=False,
    )
```

```python
import jax
import jax.numpy as jnp
from jax import lax
from jax.experimental import pallas as pl
from jax.experimental.pallas import tpu as pltpu
from jax.sharding import PartitionSpec as P

N = 256
D = 8192
TOK = 256
ROWS = 544
CUT = 272
ORDER = (
    (1, 4), (0, 1), (0, 3), (1, 12), (0, 4), (1, 1),
    (1, 3), (0, 12), (0, 5), (1, 5), (1, 7), (0, 13),
    (0, 7), (0, 2), (1, 15), (0, 15), (0, 8), (1, 13),
    (1, 8), (1, 14), (0, 9), (1, 2), (0, 14), (1, 11),
    (0, 6), (1, 6), (0, 11), (1, 10), (1, 9), (0, 10),
)
MESH = pl.DeviceIdType.MESH
f32 = jnp.float32
bf16 = jnp.bfloat16

beta_one = 0.9
beta_two = 0.95
adam_eps = 1e-08
adam_step = 100
highest = lax.Precision.HIGHEST

HPC = 2
LAG = 4
CH = 32 // HPC
CR = HPC * 64
PIECES = [(i, j) for i in range(4) for j in range(4)]


def origin(half, piece):
    sz, sy = piece
    if half == 0:
        if sz == 0:
            return (0, 1) if sy in (1, 2) else (0, -1)
        if sz == 2:
            return (1, 0) if sy in (0, 1) else (-1, 0)
        return (1, 0) if sz == 1 else (-1, 0)
    if sy == 0:
        return (1, 0) if sz == 1 else (-1, 0)
    if sy == 2:
        return (0, 1) if sz in (0, 1) else (0, -1)
    return (0, 1) if sy == 1 else (0, -1)


def children(half, piece):
    found = []
    for other in PIECES:
        if other == (0, 0):
            continue
        ez, ey = origin(half, other)
        if ((other[0] - ez) % 4, (other[1] - ey) % 4) == piece:
            found.append(((-ez, -ey), other))
    return found


def place():
    dp, y, x = lax.axis_index("dp"), lax.axis_index("context"), lax.axis_index("tensor")
    return dp // 2, dp % 2, y, x


def shifted(z, c, y, x, dz=0, dy=0, dx=0):
    return (((z + dz + 4) % 4) * 2 + c, (y + dy + 4) % 4, (x + dx + 4) % 4)


def greet(devices):
    barrier = pltpu.get_barrier_semaphore()
    for device in devices:
        pl.semaphore_signal(barrier, inc=1, device_id=device, device_id_type=MESH)
    pl.semaphore_wait(barrier, len(devices))


def half_rows(half):
    return pl.ds(half * CUT, CUT)


def columns(start, size):
    return pl.ds(pl.multiple_of(start, size), size)


def row_half(half):
    return slice(half * CUT, (half + 1) * CUT)


def rows_at(start, size):
    return pl.ds(pl.multiple_of(start, size), size)


def adam_direction(grad, moment, second):
    moment = beta_one * moment + (1.0 - beta_one) * grad
    second = beta_two * second + (1.0 - beta_two) * grad * grad
    corrected = moment / (1.0 - beta_one**adam_step)
    return corrected / (jnp.sqrt(second / (1.0 - beta_two**adam_step)) + adam_eps)


def layer_kernel(
    hidden, inputs, upstream, pw, dw, rate, step_bias, pm, ps, dmo, dse, docs, counts,
    dx_out, hid_out, pu_out, du_out, small_out,
    W, H, WX, acc, part, projected, raw, x_in, g_in, mom, sec,
    XT, GT, A, FB, zin, UV, Y, dx, mask, score, dscore, dvec, vec,
    delta_s, tail_s, head_s, logs_s, keep_s, td_s, lcol, rcol, csum, qsum, xvsum, gusum, lsum,
    rate_s, WRX, sendbuf, rbuf, small, sib_small, y_small, z_small,
    load_sem, hload_sem, hsend, hrecv, wsend, wrecv, psend, precv, xsend, xrecv, in_sem, m_sem,
    ssem, rsem, dx_sem, wxsend, wxrecv, fsend, frecv, gsend, grecv, rsend, rrecv, csend, crecv,
):
    z, c, y, x = place()
    other = 1 - c
    sibling = (z * 2 + other, y, x)
    turn_way = 1 - 2 * c

    def remote(src, dst, send_sem, recv_sem, device):
        return pltpu.make_async_remote_copy(
            src_ref=src, dst_ref=dst, send_sem=send_sem, recv_sem=recv_sem,
            device_id=device, device_id_type=MESH,
        )

    started = []

    def go(copy):
        copy.start()
        started.append(copy)
        return copy

    def slot(piece):
        return ((z + turn_way * piece[0] + 4) % 4) * 4 + (y + turn_way * piece[1] + 4) % 4

    mine = slot((0, 0))
    loads = [
        pltpu.make_async_copy(pw, W.at[mine, pl.ds(0, 512)], load_sem.at[0]),
        pltpu.make_async_copy(dw, W.at[mine, pl.ds(512, 32)], load_sem.at[1]),
    ]
    hloads = [
        pltpu.make_async_copy(
            hidden.at[0, :, columns((2 * k + c) * 1024, 1024)],
            H.at[c, :, pl.ds(k * 1024, 1024)],
            hload_sem.at[k],
        )
        for k in range(4)
    ]
    in_loads = [
        pltpu.make_async_copy(inputs.at[0], x_in, in_sem.at[0]),
        pltpu.make_async_copy(upstream.at[0], g_in, in_sem.at[1]),
    ]
    m_loads = [
        pltpu.make_async_copy(pm, mom.at[pl.ds(0, 512)], m_sem.at[0]),
        pltpu.make_async_copy(dmo, mom.at[pl.ds(512, 32)], m_sem.at[1]),
        pltpu.make_async_copy(ps, sec.at[pl.ds(0, 512)], m_sem.at[2]),
        pltpu.make_async_copy(dse, sec.at[pl.ds(512, 32)], m_sem.at[3]),
    ]
    for copy in loads + hloads + in_loads + m_loads:
        copy.start()
    greet(
        [sibling]
        + [shifted(z, c, y, x, dz=s) for s in (1, 2, 3)]
        + [shifted(z, c, y, x, dy=s) for s in (1, 2, 3)]
        + [shifted(z, c, y, x, dx=s) for s in (1, 2, 3)]
    )
    for copy in loads:
        copy.wait()

    def gathered(half, index, name, device):
        part_ref = W.at[index, half_rows(half)]
        m = name[0] * 4 + name[1]
        return remote(part_ref, part_ref, wsend.at[half, m], wrecv.at[half, m], device)

    def relay(half, piece, axis=None):
        for (ez, ey), name in children(half, piece):
            if axis is None or (axis == 0) == (ez != 0):
                go(gathered(half, slot(piece), name, shifted(z, c, y, x, dz=turn_way * ez, dy=turn_way * ey)))

    def across(index, source, group):
        return remote(
            W.at[index], WX.at[source, index % 4],
            xsend.at[index], xrecv.at[source, index % 4], (z * 2 + c, y, group),
        )

    def complete(piece):
        index = slot(piece)
        group = (z + turn_way * piece[0] + 4) % 4

        @pl.when(group != x)
        def _():
            across(index, x, group).start()

    def multiply(piece):
        index = slot(piece)
        for r in range(2):
            acc[r] += lax.dot_general(
                H[r, :, columns(index * 256, 256)], W[index],
                (((1,), (1,)), ((), ())), preferred_element_type=f32,
            )

    relay(0, (0, 0), 1)
    relay(1, (0, 0), 0)
    relay(0, (0, 0), 0)
    relay(1, (0, 0), 1)
    hremote = []
    for k in range(4):
        hremote.append(go(remote(
            hidden.at[0, :, columns((2 * k + other) * 1024, 1024)],
            H.at[c, :, pl.ds(k * 1024, 1024)], hsend.at[k], hrecv.at[k], sibling,
        )))
    complete((0, 0))

    base = y * TOK
    count = counts[0, 0]
    starts = []
    at = jnp.int32(0)
    for k in range(4):
        starts.append(at)
        at = at + docs[0, k]

    def marks(position):
        total = jnp.zeros(position.shape, jnp.int32)
        for s in starts:
            total = total + jnp.where((s >= base) & (position >= s - base), 1, 0)
        return total

    tok_row = lax.broadcasted_iota(jnp.int32, (32, TOK), 1)
    t_at = lax.broadcasted_iota(jnp.int32, (TOK, TOK), 0)
    s_at = lax.broadcasted_iota(jnp.int32, (TOK, TOK), 1)
    def turn(p, _):
        cols = columns(p * 128, 128)
        XT[rows_at(p * 128, 128), :] = x_in[:, cols].T
        GT[rows_at(p * 128, 128), :] = g_in[:, cols].T
        return 0

    def turn_all():
        for copy in in_loads:
            copy.wait()
        lax.fori_loop(0, 16, turn, 0)

    near = y // 2
    far = 1 - near
    inner = (y == 1) | (y == 2)

    def clear():
        inside = (t_at >= s_at) & (marks(t_at) == marks(s_at)) & (t_at < count)
        mask[...] = jnp.where(inside, 0.0, -1e30).astype(f32)
        dvec[...] = jnp.zeros_like(dvec)
        dscore[...] = jnp.zeros_like(dscore)

        @pl.when(jnp.logical_not(inner))
        def _():
            zin[near] = jnp.zeros((2048, N), bf16)
            UV[near] = jnp.zeros((2048, TOK), f32)

    acc[...] = jnp.zeros_like(acc)
    seen = {}
    ready = False
    for event, (half, m) in enumerate(ORDER):
        piece = (m // 4, m % 4)
        gathered(half, slot(piece), piece, sibling).wait_recv()
        relay(half, piece)
        seen[m] = seen.get(m, 0) + 1
        if seen[m] == 2:
            complete(piece)
            if not ready:
                for copy in hloads:
                    copy.wait()
                for copy in hremote:
                    copy.wait_recv()
                multiply((0, 0))
                ready = True
            multiply(piece)
        if event == 3:
            turn_all()
        if event == 11:
            clear()
    exchange = go(remote(acc.at[other], part, psend, precv, sibling))
    exchange.wait_recv()
    total_acc = acc[c] + part[...]
    projected[...] = total_acc[:, :512].astype(bf16)
    raw[...] = total_acc[:, 512:] + step_bias[...]

    def onward(way):
        return shifted(z, c, y, x, dy=1 - 2 * way)

    marks_row = marks(tok_row)
    marks_last = marks(jnp.full((32, TOK), TOK - 1, jnp.int32))
    valid_row = jnp.where(tok_row < count, 1.0, 0.0).astype(f32)
    up_to = jnp.where(t_at <= s_at, 1.0, 0.0).astype(f32)
    raw_t = raw[...].T
    rate_s[...] = jnp.broadcast_to(rate[...], (128, 32)).T
    rate_col = rate_s[:, 0:1]
    delta = valid_row * (jnp.maximum(raw_t, 0.0) + jnp.log1p(jnp.exp(-jnp.abs(raw_t))))
    logs = jnp.dot(-rate_col * delta, up_to, precision=highest, preferred_element_type=f32)
    last = logs[:, TOK - 1:TOK]
    tail = jnp.where(marks_row == marks_last, jnp.exp(last - logs), 0.0)
    head = jnp.where(marks_row == 0, jnp.exp(logs), 0.0) * valid_row
    keep = jnp.where(marks_last == 0, jnp.exp(jnp.broadcast_to(last, (32, TOK))), 0.0)
    delta_s[...] = delta
    tail_s[...] = tail
    head_s[...] = head
    logs_s[...] = logs
    keep_s[...] = keep
    td_s[...] = tail * delta
    writes, reads = projected[:, 0:N], projected[:, N:2 * N]
    vec[0] = reads
    vec[1] = writes

    def send(way, i):
        return remote(
            FB.at[way, rows_at(i * CR, CR)], zin.at[way, rows_at(i * CR, CR)],
            ssem.at[way, i], rsem.at[way, i], onward(way),
        )

    def ends(i, _):
        for j in range(HPC):
            r = rows_at(i * CR + j * 64, 64)
            h = pl.ds(HPC * i + j, 1)
            A[0, r, :] = (GT[r, :].astype(f32) * head_s[h, :]).astype(bf16)
            A[1, r, :] = (XT[r, :].astype(f32) * td_s[h, :]).astype(bf16)
        rc = rows_at(i * CR, CR)
        FB[0, rc, :] = jnp.dot(A[1, rc, :], writes, preferred_element_type=f32).astype(bf16)
        FB[1, rc, :] = jnp.dot(A[0, rc, :], reads, preferred_element_type=f32).astype(bf16)

        @pl.when(jnp.logical_not(inner))
        def _():
            send(near, i).start()

        return 0

    lax.fori_loop(0, CH, ends, 0)
    logs_col = logs.T
    for i in range(CH):
        lcol[i] = logs_col[:, HPC * i:HPC * i + HPC]
    score[...] = lax.dot_general(
        reads, writes, (((1,), (1,)), ((), ())), preferred_element_type=f32
    )

    def local(i):
        for pair in range(HPC // 2):
            cols = columns(i * CR + pair * 128, 128)
            zero = jnp.zeros((64, TOK), bf16)
            for own in range(2):
                j = pair * 2 + own
                r = rows_at(i * CR + j * 64, 64)
                h = pl.ds(HPC * i + j, 1)
                xh = XT[r, :]
                xm = jnp.concatenate([xh, zero] if own == 0 else [zero, xh], axis=0)
                lrow, drow = logs_s[h, :], delta_s[h, :]
                sums = None
                grads = None
                for t0, width in ((128, 256), (0, 128)):
                    t = slice(t0, t0 + 128)
                    gap = lcol[i, t, j:j + 1] - lrow[:, :width] + mask[t, :width]
                    decay = jnp.exp(gap)
                    dm = jnp.dot(g_in[t, cols], xm[:, :width], preferred_element_type=f32)
                    pulled = dm * decay * drow[:, :width]
                    dscore[t, :width] += pulled
                    sc = score[t, :width]
                    e = pulled * sc
                    rcol[i, t, j:j + 1] = jnp.sum(e, axis=1, keepdims=True)
                    es = jnp.sum(e, axis=0, keepdims=True)
                    mixed = jnp.dot(
                        GT[r, t], (sc * decay).astype(bf16), preferred_element_type=f32
                    )
                    if t0:
                        sums, grads = es, mixed
                        Y[r, 128:] = mixed[:, 128:]
                    else:
                        csum[h, :] = jnp.concatenate([sums[:, :128] + es, sums[:, 128:]], axis=1)
                        Y[r, :128] = grads[:, :128] + mixed

    def forward(way, i):
        for j in range(HPC):
            r = rows_at(i * CR + j * 64, 64)
            h = pl.ds(HPC * i + j, 1)
            FB[way, r, :] = (
                FB[way, r, :].astype(f32) + keep_s[h, :] * zin[way, r, :].astype(f32)
            ).astype(bf16)
        send(way, i).start()

    def state_terms(way, i):
        rc = rows_at(i * CR, CR)
        state = zin[way, rc, :]
        UV[way, rc, :] = lax.dot_general(
            state, vec[way], (((1,), (1,)), ((), ())), preferred_element_type=f32
        )
        dvec[way] += lax.dot_general(
            A[way, rc, :], state, (((0,), (0,)), ((), ())), preferred_element_type=f32
        )

    def finish(i):
        for pair in range(HPC // 2):
            for own in range(2):
                j = pair * 2 + own
                r = rows_at(i * CR + j * 64, 64)
                h = pl.ds(HPC * i + j, 1)
                v = UV[1, r, :]
                xt = XT[r, :].astype(f32)
                yt = Y[r, :] + tail_s[h, :] * v
                qsum[h, :] = jnp.sum(xt * yt, axis=0, keepdims=True)
                xvsum[h, :] = jnp.sum(xt * v, axis=0, keepdims=True)
                gusum[h, :] = jnp.sum(GT[r, :].astype(f32) * UV[0, r, :], axis=0, keepdims=True)
                lsum[h, :] = jnp.sum(
                    zin[0, r, :].astype(f32) * zin[1, r, :].astype(f32), axis=0, keepdims=True
                )
                Y[r, :] = delta_s[h, :] * yt
            rp = rows_at(i * CR + pair * 128, 128)
            dx[:, columns(i * CR + pair * 128, 128)] = Y[rp, :].astype(bf16).T

    def step(k, _):
        @pl.when(k < CH)
        def _():
            local(k)

            @pl.when(inner)
            def _():
                send(near, k).wait_recv()
                forward(near, k)
                state_terms(near, k)

        @pl.when(k >= LAG)
        def _():
            i = k - LAG
            send(far, i).wait_recv()

            @pl.when(inner)
            def _():
                forward(far, i)

            state_terms(far, i)
            finish(i)

        return 0

    lax.fori_loop(0, CH + LAG, step, 0)
    dx_copy = pltpu.make_async_copy(dx, dx_out, dx_sem)
    dx_copy.start()

    rows = jnp.concatenate([rcol[i] for i in range(CH)], axis=1).T
    pulls = td_s[...] * xvsum[...]
    change = rows - csum[...] + head_s[...] * gusum[...] - pulls
    at_end = jnp.sum(pulls + keep_s[...] * lsum[...], axis=1, keepdims=True)
    tok_row = lax.broadcasted_iota(jnp.int32, (32, TOK), 1)
    change = change + jnp.where(tok_row == TOK - 1, at_end, 0.0)
    t_at = lax.broadcasted_iota(jnp.int32, (TOK, TOK), 0)
    s_at = lax.broadcasted_iota(jnp.int32, (TOK, TOK), 1)
    down_to = jnp.where(t_at >= s_at, 1.0, 0.0).astype(f32)
    dlog = jnp.dot(change, down_to, precision=highest, preferred_element_type=f32)
    ddelta = qsum[...] - rate_s[:, 0:1] * dlog
    raw_t = raw[...].T
    valid_row = jnp.where(tok_row < count, 1.0, 0.0).astype(f32)
    raw_grad = ddelta * valid_row * (1.0 / (1.0 + jnp.exp(-raw_t)))
    rate_grad = jnp.sum(-delta_s[...] * dlog, axis=1, keepdims=True)
    bias_grad = jnp.sum(raw_grad, axis=1, keepdims=True)
    lane = lax.broadcasted_iota(jnp.int32, (32, 128), 1)
    small[...] = jnp.where(
        lane == 0, rate_grad, jnp.where(lane == 1, bias_grad, count.astype(f32))
    )
    ds = dscore[...].astype(bf16)
    WRX[x, c, :, 0:N] = (
        dvec[1]
        + lax.dot_general(ds, vec[0], (((0,), (0,)), ((), ())), preferred_element_type=f32)
    ).astype(bf16)
    WRX[x, c, :, N:2 * N] = (
        dvec[0] + jnp.dot(ds, vec[1], preferred_element_type=f32)
    ).astype(bf16)
    WRX[x, c, :, 2 * N:] = raw_grad.T.astype(bf16)

    def wr_to(group, device, send_index, recv_index):
        return remote(
            WRX.at[group, c], WRX.at[group, c], wxsend.at[send_index], wxrecv.at[recv_index], device
        )

    own_wr = go(wr_to(x, sibling, 0, 0))
    for s in (1, 3, 2):
        go(wr_to(x, shifted(z, c, y, x, dx=s), s, s))
    s_copy = go(remote(small, sib_small, csend.at[0], crecv.at[0], sibling))
    own_wr.wait_recv()

    def product(m):
        index = slot((m // 4, m % 4))
        value = lax.dot_general(
            WRX[x, 0], H[0, :, columns(index * 256, 256)], (((0,), (0,)), ((), ())),
            preferred_element_type=f32,
        )
        value += lax.dot_general(
            WRX[x, 1], H[1, :, columns(index * 256, 256)], (((0,), (0,)), ((), ())),
            preferred_element_type=f32,
        )
        sendbuf[m] = value.astype(bf16)

    def reduced(half, src, m, device):
        return remote(
            sendbuf.at[src, half_rows(half)], rbuf.at[half, m],
            gsend.at[half, m], grecv.at[half, m], device,
        )

    def up(half, m):
        ez, ey = origin(half, (m // 4, m % 4))
        go(reduced(half, m, m, shifted(z, c, y, x, dz=turn_way * ez, dy=turn_way * ey)))

    def total(half, m):
        value = sendbuf[m, row_half(half)].astype(f32)
        for _, name in children(half, (m // 4, m % 4)):
            k = name[0] * 4 + name[1]
            reduced(half, m, k, sibling).wait_recv()
            value = value + rbuf[half, k].astype(f32)
        return value

    done = set()
    climb = []
    for half, m in reversed(ORDER):
        if m not in done:
            product(m)
            done.add(m)
        if children(half, (m // 4, m % 4)):
            climb.append((half, m))
        else:
            up(half, m)
    product(0)

    s_copy.wait_recv()
    y_small[y] = small[...] + sib_small[...]
    for s in (1, 2, 3):
        go(remote(
            y_small.at[y], y_small.at[y], csend.at[s], crecv.at[s], shifted(z, c, y, x, dy=s)
        ))

    def small_z():
        for s in (1, 2, 3):
            remote(
                y_small.at[y], y_small.at[(y - s + 4) % 4], csend.at[s], crecv.at[s], sibling
            ).wait_recv()
        z_small[z] = (y_small[0] + y_small[1]) + (y_small[2] + y_small[3])
        for s in (1, 2, 3):
            go(remote(
                z_small.at[z], z_small.at[z], csend.at[3 + s], crecv.at[3 + s],
                shifted(z, c, y, x, dz=s),
            ))

    def small_end():
        for s in (1, 2, 3):
            remote(
                z_small.at[z], z_small.at[(z - s + 4) % 4], csend.at[3 + s], crecv.at[3 + s], sibling
            ).wait_recv()
        small_out[...] = (z_small[0] + z_small[1]) + (z_small[2] + z_small[3])

    def tile(r, k):
        return pl.ds((r * 4 + k) * 256, 256)

    def hidden_own():
        for r in range(2):
            for k in range(4):
                Y[tile(r, k), :] = jnp.dot(WRX[x, r], W[x * 4 + k], preferred_element_type=f32)

    def pass_on(s):
        group = (x - s + 4) % 4
        remote(
            WRX.at[group, c], WRX.at[group, c], wxsend.at[s], wxrecv.at[s], sibling
        ).wait_recv()
        go(remote(WRX.at[group, c], WRX.at[group, c], fsend.at[s], frecv.at[s], sibling))

    def hidden_add(s):
        group = (x - s + 4) % 4
        remote(
            WRX.at[group, other], WRX.at[group, other], fsend.at[s], frecv.at[s], sibling
        ).wait_recv()
        for k in range(4):
            remote(
                W.at[0], WX.at[group, k], xsend.at[0], xrecv.at[group, k], sibling
            ).wait_recv()
        for r in range(2):
            for k in range(4):
                Y[tile(r, k), :] += jnp.dot(
                    WRX[group, r], WX[group, k], preferred_element_type=f32
                )

    def hidden_end():
        for r in range(2):
            for k in range(4):
                XT[tile(r, k), :] = Y[tile(r, k), :].astype(bf16)
        for k in range(4):
            go(remote(
                XT.at[pl.ds((other * 4 + k) * 256, 256)],
                hid_out.at[:, columns(c * 1024 + k * 256, 256)],
                rsend.at[k], rrecv.at[k], sibling,
            ))
        for k in range(4):
            hid_out[:, columns(c * 1024 + k * 256, 256)] = XT[rows_at((c * 4 + k) * 256, 256), :]

    hidden_own()
    small_z()
    beside = {
        4: lambda: pass_on(1), 5: lambda: pass_on(3), 6: lambda: pass_on(2),
        8: lambda: hidden_add(1), 10: lambda: hidden_add(3), 12: lambda: hidden_add(2),
        13: hidden_end,
    }
    for step_at, (half, m) in enumerate(climb):
        sendbuf[m, row_half(half)] = total(half, m).astype(bf16)
        up(half, m)
        if step_at in beside:
            beside[step_at]()
    small_end()
    sums = small_out[...]
    small_out[...] = sums / sums[:, 2:3]
    tokens = sums[0:1, 2:3]
    for copy in m_loads:
        copy.wait()
    first = adam_direction(total(0, 0) / tokens, mom[row_half(0)], sec[row_half(0)])
    pu_out[0:CUT] = first
    second = adam_direction(total(1, 0) / tokens, mom[row_half(1)], sec[row_half(1)])
    pu_out[CUT:512] = second[:512 - CUT]
    du_out[...] = second[512 - CUT:]
    for k in range(4):
        remote(
            XT.at[pl.ds(k * 256, 256)], hid_out.at[:, columns(other * 1024 + k * 256, 256)],
            rsend.at[k], rrecv.at[k], sibling,
        ).wait_recv()

    for copy in started:
        copy.wait_send()
    for k in range(16):
        @pl.when(k // 4 != x)
        def _():
            across(k, x, k // 4).wait_send()

    def drain(i, _):
        send(near, i).wait_send()

        @pl.when(inner)
        def _():
            send(far, i).wait_send()

        return 0

    lax.fori_loop(0, CH, drain, 0)
    dx_copy.wait()


VM = pl.BlockSpec(memory_space=pltpu.VMEM)
ANY = pl.BlockSpec(memory_space=pl.ANY)
SM = pl.BlockSpec(memory_space=pltpu.SMEM)
DMA = pltpu.SemaphoreType.DMA


def emit_kernel(
    dx, hid, pu, du, sums, dx_out, hid_out, pu_out, du_out, rate_out, bias_out
):
    dx_out[...] = dx[...]
    hid_out[...] = hid[...]
    pu_out[...] = pu[...]
    du_out[...] = du[...]
    turned = sums[...].T
    rate_out[...] = turned[0:1]
    bias_out[...] = turned[1:2]


def shards(
    hidden,
    inputs,
    upstream,
    proj_weight,
    delta_weight,
    decay_rate,
    step_bias,
    proj_moment,
    proj_second,
    delta_moment,
    delta_second,
    doc_lengths,
    valid_counts,
):
    def vmem(shape, dtype=f32):
        return pltpu.VMEM(shape, dtype)

    row = vmem((32, TOK))
    input_grad, hidden_grad, proj_update, delta_update, sums = pl.pallas_call(
        layer_kernel,
        out_shape=(
            jax.ShapeDtypeStruct((TOK, 2048), bf16),
            jax.ShapeDtypeStruct((TOK, 2048), bf16),
            jax.ShapeDtypeStruct((512, 256), f32),
            jax.ShapeDtypeStruct((32, 256), f32),
            jax.ShapeDtypeStruct((32, 128), f32),
        ),
        in_specs=[ANY, ANY, ANY, ANY, ANY, VM, VM, ANY, ANY, ANY, ANY, SM, SM],
        out_specs=(ANY, VM, VM, VM, VM),
        scratch_shapes=[
            vmem((16, ROWS, 256), bf16),
            vmem((2, TOK, D // 2), bf16),
            vmem((4, 4, ROWS, 256), bf16),
            vmem((2, TOK, ROWS)),
            vmem((TOK, ROWS)),
            vmem((TOK, 512), bf16),
            vmem((TOK, 32)),
            vmem((TOK, 2048), bf16),
            vmem((TOK, 2048), bf16),
            vmem((ROWS, 256)),
            vmem((ROWS, 256)),
            vmem((2048, TOK), bf16),
            vmem((2048, TOK), bf16),
            vmem((2, 2048, TOK), bf16),
            vmem((2, 2048, N), bf16),
            vmem((2, 2048, N), bf16),
            vmem((2, 2048, TOK)),
            vmem((2048, TOK)),
            vmem((TOK, 2048), bf16),
            vmem((TOK, TOK)),
            vmem((TOK, TOK)),
            vmem((TOK, TOK)),
            vmem((2, TOK, N)),
            vmem((2, TOK, N), bf16),
            row, row, row, row, row, row,
            vmem((CH, TOK, HPC)),
            vmem((CH, TOK, HPC)),
            row, row, row, row, row,
            vmem((32, 128)),
            vmem((4, 2, TOK, ROWS), bf16),
            vmem((16, ROWS, 256), bf16),
            vmem((2, 16, CUT, 256), bf16),
            vmem((32, 128)), vmem((32, 128)), vmem((4, 32, 128)), vmem((4, 32, 128)),
            DMA((2,)), DMA((4,)), DMA((4,)), DMA((4,)), DMA((2, 16)), DMA((2, 16)), DMA, DMA,
            DMA((16,)), DMA((4, 4)), DMA((2,)), DMA((4,)),
            DMA((2, CH)), DMA((2, CH)), DMA, DMA((4,)), DMA((4,)), DMA((4,)), DMA((4,)),
            DMA((2, 16)), DMA((2, 16)), DMA((4,)), DMA((4,)), DMA((7,)), DMA((7,)),
        ],
        compiler_params=pltpu.CompilerParams(
            collective_id=0, has_side_effects=True, vmem_limit_bytes=60 * 2**20
        ),
        name="layer_backward",
    )(
        hidden, inputs, upstream, proj_weight, delta_weight, decay_rate.reshape(1, 32),
        step_bias.reshape(1, 32), proj_moment, proj_second, delta_moment, delta_second,
        doc_lengths, valid_counts,
    )
    held = (input_grad, hidden_grad, proj_update, delta_update)
    line = jax.ShapeDtypeStruct((1, 32), f32)
    blocks = [pl.BlockSpec((a.shape[0] // 2, a.shape[1]), lambda i: (i, 0)) for a in held]
    input_grad, hidden_grad, proj_update, delta_update, rate_grad, bias_grad = pl.pallas_call(
        emit_kernel,
        out_shape=tuple(jax.ShapeDtypeStruct(a.shape, a.dtype) for a in held) + (line, line),
        grid=(2,),
        in_specs=blocks + [pl.BlockSpec((32, 128), lambda i: (0, 0))],
        out_specs=tuple(blocks) + (pl.BlockSpec((1, 32), lambda i: (0, 0)),) * 2,
        name="emit",
    )(*held, sums)
    return (
        input_grad[None], hidden_grad[None], rate_grad[0], bias_grad[0], proj_update, delta_update
    )


def solution(mesh):
    return jax.shard_map(
        shards,
        mesh=mesh,
        in_specs=(
            P("dp", "context", None),
            P("dp", "context", "tensor"),
            P("dp", "context", "tensor"),
            P("tensor", ("dp", "context")),
            P("tensor", ("dp", "context")),
            P("tensor"),
            P("tensor"),
            P("tensor", ("dp", "context")),
            P("tensor", ("dp", "context")),
            P("tensor", ("dp", "context")),
            P("tensor", ("dp", "context")),
            P("dp", None),
            P("dp", "context"),
        ),
        out_specs=(
            P("dp", "context", "tensor"),
            P("dp", "context", "tensor"),
            P("tensor"),
            P("tensor"),
            P("tensor", ("dp", "context")),
            P("tensor", ("dp", "context")),
        ),
        check_vma=False,
    )
```

```python
import jax
import jax.numpy as jnp
from jax import lax
from jax.experimental import pallas as pl
from jax.experimental.pallas import tpu as pltpu
from jax.sharding import PartitionSpec as P

N = 256
D = 8192
TOK = 256
ROWS = 544
CUT = 272
ORDER = (
    (1, 4), (0, 1), (0, 3), (1, 12), (0, 4), (1, 1),
    (1, 3), (0, 12), (0, 5), (1, 5), (1, 7), (0, 13),
    (0, 7), (0, 2), (1, 15), (0, 15), (0, 8), (1, 13),
    (1, 8), (1, 14), (0, 9), (1, 2), (0, 14), (1, 11),
    (0, 6), (1, 6), (0, 11), (1, 10), (1, 9), (0, 10),
)
MESH = pl.DeviceIdType.MESH
f32 = jnp.float32
bf16 = jnp.bfloat16

beta_one = 0.9
beta_two = 0.95
adam_eps = 1e-08
adam_step = 100
highest = lax.Precision.HIGHEST

HPC = 2
LAG = 3
CH = 32 // HPC
CR = HPC * 64
PIECES = [(i, j) for i in range(4) for j in range(4)]


def origin(half, piece):
    sz, sy = piece
    if half == 0:
        if sz == 0:
            return (0, 1) if sy in (1, 2) else (0, -1)
        if sz == 2:
            return (1, 0) if sy in (0, 1) else (-1, 0)
        return (1, 0) if sz == 1 else (-1, 0)
    if sy == 0:
        return (1, 0) if sz == 1 else (-1, 0)
    if sy == 2:
        return (0, 1) if sz in (0, 1) else (0, -1)
    return (0, 1) if sy == 1 else (0, -1)


def children(half, piece):
    found = []
    for other in PIECES:
        if other == (0, 0):
            continue
        ez, ey = origin(half, other)
        if ((other[0] - ez) % 4, (other[1] - ey) % 4) == piece:
            found.append(((-ez, -ey), other))
    return found


def place():
    dp, y, x = lax.axis_index("dp"), lax.axis_index("context"), lax.axis_index("tensor")
    return dp // 2, dp % 2, y, x


def shifted(z, c, y, x, dz=0, dy=0, dx=0):
    return (((z + dz + 4) % 4) * 2 + c, (y + dy + 4) % 4, (x + dx + 4) % 4)


def greet(devices):
    barrier = pltpu.get_barrier_semaphore()
    for device in devices:
        pl.semaphore_signal(barrier, inc=1, device_id=device, device_id_type=MESH)
    pl.semaphore_wait(barrier, len(devices))


def half_rows(half):
    return pl.ds(half * CUT, CUT)


def columns(start, size):
    return pl.ds(pl.multiple_of(start, size), size)


def row_half(half):
    return slice(half * CUT, (half + 1) * CUT)


def rows_at(start, size):
    return pl.ds(pl.multiple_of(start, size), size)


def adam_direction(grad, moment, second):
    moment = beta_one * moment + (1.0 - beta_one) * grad
    second = beta_two * second + (1.0 - beta_two) * grad * grad
    corrected = moment / (1.0 - beta_one**adam_step)
    return corrected / (jnp.sqrt(second / (1.0 - beta_two**adam_step)) + adam_eps)


def layer_kernel(
    hidden, inputs, upstream, pw, dw, rate, step_bias, pm, ps, dmo, dse, docs, counts,
    dx_out, hid_out, pu_out, du_out, small_out,
    W, H, WX, acc, part, projected, raw, x_in, g_in, mom, sec,
    XT, GT, A, FB, zin, UV, Y, dx, mask, score, dscore, dvec, vec,
    delta_s, tail_s, head_s, logs_s, keep_s, td_s, lcol, rcol, csum, qsum, xvsum, gusum, lsum,
    rate_s, WRX, sendbuf, rbuf, small, sib_small, y_small, z_small,
    load_sem, hload_sem, hsend, hrecv, wsend, wrecv, psend, precv, xsend, xrecv, in_sem, m_sem,
    ssem, rsem, dx_sem, wxsend, wxrecv, fsend, frecv, gsend, grecv, rsend, rrecv, csend, crecv,
):
    z, c, y, x = place()
    other = 1 - c
    sibling = (z * 2 + other, y, x)
    turn_way = 1 - 2 * c

    def remote(src, dst, send_sem, recv_sem, device):
        return pltpu.make_async_remote_copy(
            src_ref=src, dst_ref=dst, send_sem=send_sem, recv_sem=recv_sem,
            device_id=device, device_id_type=MESH,
        )

    started = []

    def go(copy):
        copy.start()
        started.append(copy)
        return copy

    def slot(piece):
        return ((z + turn_way * piece[0] + 4) % 4) * 4 + (y + turn_way * piece[1] + 4) % 4

    mine = slot((0, 0))
    loads = [
        pltpu.make_async_copy(pw, W.at[mine, pl.ds(0, 512)], load_sem.at[0]),
        pltpu.make_async_copy(dw, W.at[mine, pl.ds(512, 32)], load_sem.at[1]),
    ]
    hloads = [
        pltpu.make_async_copy(
            hidden.at[0, :, columns((2 * k + c) * 1024, 1024)],
            H.at[c, :, pl.ds(k * 1024, 1024)],
            hload_sem.at[k],
        )
        for k in range(4)
    ]
    in_loads = [
        pltpu.make_async_copy(inputs.at[0], x_in, in_sem.at[0]),
        pltpu.make_async_copy(upstream.at[0], g_in, in_sem.at[1]),
    ]
    m_loads = [
        pltpu.make_async_copy(pm, mom.at[pl.ds(0, 512)], m_sem.at[0]),
        pltpu.make_async_copy(dmo, mom.at[pl.ds(512, 32)], m_sem.at[1]),
        pltpu.make_async_copy(ps, sec.at[pl.ds(0, 512)], m_sem.at[2]),
        pltpu.make_async_copy(dse, sec.at[pl.ds(512, 32)], m_sem.at[3]),
    ]
    for copy in loads + hloads + in_loads + m_loads:
        copy.start()
    greet(
        [sibling]
        + [shifted(z, c, y, x, dz=s) for s in (1, 2, 3)]
        + [shifted(z, c, y, x, dy=s) for s in (1, 2, 3)]
        + [shifted(z, c, y, x, dx=s) for s in (1, 2, 3)]
    )
    for copy in loads:
        copy.wait()

    def gathered(half, index, name, device):
        part_ref = W.at[index, half_rows(half)]
        m = name[0] * 4 + name[1]
        return remote(part_ref, part_ref, wsend.at[half, m], wrecv.at[half, m], device)

    def relay(half, piece, axis=None):
        for (ez, ey), name in children(half, piece):
            if axis is None or (axis == 0) == (ez != 0):
                go(gathered(half, slot(piece), name, shifted(z, c, y, x, dz=turn_way * ez, dy=turn_way * ey)))

    def across(index, source, group):
        return remote(
            W.at[index], WX.at[source, index % 4],
            xsend.at[index], xrecv.at[source, index % 4], (z * 2 + c, y, group),
        )

    def complete(piece):
        index = slot(piece)
        group = (z + turn_way * piece[0] + 4) % 4

        @pl.when(group != x)
        def _():
            across(index, x, group).start()

    def multiply(piece):
        index = slot(piece)
        for r in range(2):
            acc[r] += lax.dot_general(
                H[r, :, columns(index * 256, 256)], W[index],
                (((1,), (1,)), ((), ())), preferred_element_type=f32,
            )

    relay(0, (0, 0), 1)
    relay(1, (0, 0), 0)
    relay(0, (0, 0), 0)
    relay(1, (0, 0), 1)
    hremote = []
    for k in range(4):
        hremote.append(go(remote(
            hidden.at[0, :, columns((2 * k + other) * 1024, 1024)],
            H.at[c, :, pl.ds(k * 1024, 1024)], hsend.at[k], hrecv.at[k], sibling,
        )))
    complete((0, 0))

    base = y * TOK
    count = counts[...]
    starts = []
    at = jnp.zeros((1, 1), jnp.int32)
    for k in range(4):
        starts.append(at)
        at = at + docs[:, k:k + 1]

    def marks(position):
        total = jnp.zeros(position.shape, jnp.int32)
        for s in starts:
            total = total + jnp.where((s >= base) & (position >= s - base), 1, 0)
        return total

    tok_row = lax.broadcasted_iota(jnp.int32, (32, TOK), 1)
    t_at = lax.broadcasted_iota(jnp.int32, (TOK, TOK), 0)
    s_at = lax.broadcasted_iota(jnp.int32, (TOK, TOK), 1)
    def turn(p, _):
        cols = columns(p * 128, 128)
        XT[rows_at(p * 128, 128), :] = x_in[:, cols].T
        GT[rows_at(p * 128, 128), :] = g_in[:, cols].T
        return 0

    def turn_all():
        for copy in in_loads:
            copy.wait()
        lax.fori_loop(0, 16, turn, 0)

    near = y // 2
    far = 1 - near
    inner = (y == 1) | (y == 2)

    def clear():
        inside = (t_at >= s_at) & (marks(t_at) == marks(s_at)) & (t_at < count)
        mask[...] = jnp.where(inside, 0.0, -1e30).astype(f32)
        dvec[...] = jnp.zeros_like(dvec)
        dscore[...] = jnp.zeros_like(dscore)

        @pl.when(jnp.logical_not(inner))
        def _():
            zin[near] = jnp.zeros((2048, N), bf16)
            UV[near] = jnp.zeros((2048, TOK), f32)

    acc[...] = jnp.zeros_like(acc)
    seen = {}
    ready = False
    for event, (half, m) in enumerate(ORDER):
        piece = (m // 4, m % 4)
        gathered(half, slot(piece), piece, sibling).wait_recv()
        relay(half, piece)
        seen[m] = seen.get(m, 0) + 1
        if seen[m] == 2:
            complete(piece)
            if not ready:
                for copy in hloads:
                    copy.wait()
                for copy in hremote:
                    copy.wait_recv()
                multiply((0, 0))
                ready = True
            multiply(piece)
        if event == 3:
            turn_all()
        if event == 11:
            clear()
    exchange = go(remote(acc.at[other], part, psend, precv, sibling))
    exchange.wait_recv()
    total_acc = acc[c] + part[...]
    projected[...] = total_acc[:, :512].astype(bf16)
    raw[...] = total_acc[:, 512:] + step_bias[...]

    def onward(way):
        return shifted(z, c, y, x, dy=1 - 2 * way)

    marks_row = marks(tok_row)
    marks_last = marks(jnp.full((32, TOK), TOK - 1, jnp.int32))
    valid_row = jnp.where(tok_row < count, 1.0, 0.0).astype(f32)
    up_to = jnp.where(t_at <= s_at, 1.0, 0.0).astype(f32)
    raw_t = raw[...].T
    rate_s[...] = jnp.broadcast_to(rate[...], (128, 32)).T
    rate_col = rate_s[:, 0:1]
    delta = valid_row * (jnp.maximum(raw_t, 0.0) + jnp.log1p(jnp.exp(-jnp.abs(raw_t))))
    logs = jnp.dot(-rate_col * delta, up_to, precision=highest, preferred_element_type=f32)
    last = logs[:, TOK - 1:TOK]
    tail = jnp.where(marks_row == marks_last, jnp.exp(last - logs), 0.0)
    head = jnp.where(marks_row == 0, jnp.exp(logs), 0.0) * valid_row
    keep = jnp.where(marks_last == 0, jnp.exp(jnp.broadcast_to(last, (32, TOK))), 0.0)
    delta_s[...] = delta
    tail_s[...] = tail
    head_s[...] = head
    logs_s[...] = logs
    keep_s[...] = keep
    td_s[...] = tail * delta
    writes, reads = projected[:, 0:N], projected[:, N:2 * N]
    vec[0] = reads
    vec[1] = writes

    def send(way, i):
        return remote(
            FB.at[way, rows_at(i * CR, CR)], zin.at[way, rows_at(i * CR, CR)],
            ssem.at[way, i], rsem.at[way, i], onward(way),
        )

    def ends(i, _):
        for j in range(HPC):
            r = rows_at(i * CR + j * 64, 64)
            h = pl.ds(HPC * i + j, 1)
            A[0, r, :] = (GT[r, :].astype(f32) * head_s[h, :]).astype(bf16)
            A[1, r, :] = (XT[r, :].astype(f32) * td_s[h, :]).astype(bf16)
        rc = rows_at(i * CR, CR)
        FB[0, rc, :] = jnp.dot(A[1, rc, :], writes, preferred_element_type=f32).astype(bf16)
        FB[1, rc, :] = jnp.dot(A[0, rc, :], reads, preferred_element_type=f32).astype(bf16)

        @pl.when(jnp.logical_not(inner))
        def _():
            send(near, i).start()

        return 0

    lax.fori_loop(0, CH, ends, 0)
    logs_col = logs.T
    for i in range(CH):
        lcol[i] = logs_col[:, HPC * i:HPC * i + HPC]
    score[...] = lax.dot_general(
        reads, writes, (((1,), (1,)), ((), ())), preferred_element_type=f32
    )

    def local(i):
        for pair in range(HPC // 2):
            cols = columns(i * CR + pair * 128, 128)
            zero = jnp.zeros((64, TOK), bf16)
            for own in range(2):
                j = pair * 2 + own
                r = rows_at(i * CR + j * 64, 64)
                h = pl.ds(HPC * i + j, 1)
                xh = XT[r, :]
                xm = jnp.concatenate([xh, zero] if own == 0 else [zero, xh], axis=0)
                lrow, drow = logs_s[h, :], delta_s[h, :]
                sums = None
                grads = None
                for t0, width in ((128, 256), (0, 128)):
                    t = slice(t0, t0 + 128)
                    gap = lcol[i, t, j:j + 1] - lrow[:, :width] + mask[t, :width]
                    decay = jnp.exp(gap)
                    dm = jnp.dot(g_in[t, cols], xm[:, :width], preferred_element_type=f32)
                    pulled = dm * decay * drow[:, :width]
                    dscore[t, :width] += pulled
                    sc = score[t, :width]
                    e = pulled * sc
                    rcol[i, t, j:j + 1] = jnp.sum(e, axis=1, keepdims=True)
                    es = jnp.sum(e, axis=0, keepdims=True)
                    mixed = jnp.dot(
                        GT[r, t], (sc * decay).astype(bf16), preferred_element_type=f32
                    )
                    if t0:
                        sums, grads = es, mixed
                        Y[r, 128:] = mixed[:, 128:]
                    else:
                        csum[h, :] = jnp.concatenate([sums[:, :128] + es, sums[:, 128:]], axis=1)
                        Y[r, :128] = grads[:, :128] + mixed

    def forward(way, i):
        for j in range(HPC):
            r = rows_at(i * CR + j * 64, 64)
            h = pl.ds(HPC * i + j, 1)
            FB[way, r, :] = (
                FB[way, r, :].astype(f32) + keep_s[h, :] * zin[way, r, :].astype(f32)
            ).astype(bf16)
        send(way, i).start()

    def state_terms(way, i):
        rc = rows_at(i * CR, CR)
        state = zin[way, rc, :]
        UV[way, rc, :] = lax.dot_general(
            state, vec[way], (((1,), (1,)), ((), ())), preferred_element_type=f32
        )
        dvec[way] += lax.dot_general(
            A[way, rc, :], state, (((0,), (0,)), ((), ())), preferred_element_type=f32
        )

    def finish(i):
        for pair in range(HPC // 2):
            for own in range(2):
                j = pair * 2 + own
                r = rows_at(i * CR + j * 64, 64)
                h = pl.ds(HPC * i + j, 1)
                v = UV[1, r, :]
                xt = XT[r, :].astype(f32)
                yt = Y[r, :] + tail_s[h, :] * v
                qsum[h, :] = jnp.sum(xt * yt, axis=0, keepdims=True)
                xvsum[h, :] = jnp.sum(xt * v, axis=0, keepdims=True)
                gusum[h, :] = jnp.sum(GT[r, :].astype(f32) * UV[0, r, :], axis=0, keepdims=True)
                lsum[h, :] = jnp.sum(
                    zin[0, r, :].astype(f32) * zin[1, r, :].astype(f32), axis=0, keepdims=True
                )
                Y[r, :] = delta_s[h, :] * yt
            rp = rows_at(i * CR + pair * 128, 128)
            dx[:, columns(i * CR + pair * 128, 128)] = Y[rp, :].astype(bf16).T

    def step(k, _):
        @pl.when(k < CH)
        def _():
            local(k)

            @pl.when(inner)
            def _():
                send(near, k).wait_recv()
                forward(near, k)
                state_terms(near, k)

        @pl.when(k >= LAG)
        def _():
            i = k - LAG
            send(far, i).wait_recv()

            @pl.when(inner)
            def _():
                forward(far, i)

            state_terms(far, i)
            finish(i)

        return 0

    lax.fori_loop(0, CH + LAG, step, 0)
    dx_copy = pltpu.make_async_copy(dx, dx_out, dx_sem)
    dx_copy.start()

    rows = jnp.concatenate([rcol[i] for i in range(CH)], axis=1).T
    pulls = td_s[...] * xvsum[...]
    change = rows - csum[...] + head_s[...] * gusum[...] - pulls
    at_end = jnp.sum(pulls + keep_s[...] * lsum[...], axis=1, keepdims=True)
    tok_row = lax.broadcasted_iota(jnp.int32, (32, TOK), 1)
    change = change + jnp.where(tok_row == TOK - 1, at_end, 0.0)
    t_at = lax.broadcasted_iota(jnp.int32, (TOK, TOK), 0)
    s_at = lax.broadcasted_iota(jnp.int32, (TOK, TOK), 1)
    down_to = jnp.where(t_at >= s_at, 1.0, 0.0).astype(f32)
    dlog = jnp.dot(change, down_to, precision=highest, preferred_element_type=f32)
    ddelta = qsum[...] - rate_s[:, 0:1] * dlog
    raw_t = raw[...].T
    valid_row = jnp.where(tok_row < count, 1.0, 0.0).astype(f32)
    raw_grad = ddelta * valid_row * (1.0 / (1.0 + jnp.exp(-raw_t)))
    rate_grad = jnp.sum(-delta_s[...] * dlog, axis=1, keepdims=True)
    bias_grad = jnp.sum(raw_grad, axis=1, keepdims=True)
    lane = lax.broadcasted_iota(jnp.int32, (32, 128), 1)
    small[...] = jnp.where(
        lane == 0, rate_grad, jnp.where(lane == 1, bias_grad, count.astype(f32))
    )
    ds = dscore[...].astype(bf16)
    WRX[x, c, :, 0:N] = (
        dvec[1]
        + lax.dot_general(ds, vec[0], (((0,), (0,)), ((), ())), preferred_element_type=f32)
    ).astype(bf16)
    WRX[x, c, :, N:2 * N] = (
        dvec[0] + jnp.dot(ds, vec[1], preferred_element_type=f32)
    ).astype(bf16)
    WRX[x, c, :, 2 * N:] = raw_grad.T.astype(bf16)

    def wr_to(group, device, send_index, recv_index):
        return remote(
            WRX.at[group, c], WRX.at[group, c], wxsend.at[send_index], wxrecv.at[recv_index], device
        )

    own_wr = go(wr_to(x, sibling, 0, 0))
    for s in (1, 3, 2):
        go(wr_to(x, shifted(z, c, y, x, dx=s), s, s))
    s_copy = go(remote(small, sib_small, csend.at[0], crecv.at[0], sibling))
    own_wr.wait_recv()

    def product(m):
        index = slot((m // 4, m % 4))
        value = lax.dot_general(
            WRX[x, 0], H[0, :, columns(index * 256, 256)], (((0,), (0,)), ((), ())),
            preferred_element_type=f32,
        )
        value += lax.dot_general(
            WRX[x, 1], H[1, :, columns(index * 256, 256)], (((0,), (0,)), ((), ())),
            preferred_element_type=f32,
        )
        sendbuf[m] = value.astype(bf16)

    def reduced(half, src, m, device):
        return remote(
            sendbuf.at[src, half_rows(half)], rbuf.at[half, m],
            gsend.at[half, m], grecv.at[half, m], device,
        )

    def up(half, m):
        ez, ey = origin(half, (m // 4, m % 4))
        go(reduced(half, m, m, shifted(z, c, y, x, dz=turn_way * ez, dy=turn_way * ey)))

    def total(half, m):
        value = sendbuf[m, row_half(half)].astype(f32)
        for _, name in children(half, (m // 4, m % 4)):
            k = name[0] * 4 + name[1]
            reduced(half, m, k, sibling).wait_recv()
            value = value + rbuf[half, k].astype(f32)
        return value

    done = set()
    climb = []
    for half, m in reversed(ORDER):
        if m not in done:
            product(m)
            done.add(m)
        if children(half, (m // 4, m % 4)):
            climb.append((half, m))
        else:
            up(half, m)
    product(0)

    s_copy.wait_recv()
    y_small[y] = small[...] + sib_small[...]
    for s in (1, 2, 3):
        go(remote(
            y_small.at[y], y_small.at[y], csend.at[s], crecv.at[s], shifted(z, c, y, x, dy=s)
        ))

    def small_z():
        for s in (1, 2, 3):
            remote(
                y_small.at[y], y_small.at[(y - s + 4) % 4], csend.at[s], crecv.at[s], sibling
            ).wait_recv()
        z_small[z] = (y_small[0] + y_small[1]) + (y_small[2] + y_small[3])
        for s in (1, 2, 3):
            go(remote(
                z_small.at[z], z_small.at[z], csend.at[3 + s], crecv.at[3 + s],
                shifted(z, c, y, x, dz=s),
            ))

    def small_end():
        for s in (1, 2, 3):
            remote(
                z_small.at[z], z_small.at[(z - s + 4) % 4], csend.at[3 + s], crecv.at[3 + s], sibling
            ).wait_recv()
        small_out[...] = (z_small[0] + z_small[1]) + (z_small[2] + z_small[3])

    def tile(r, k):
        return pl.ds((r * 4 + k) * 256, 256)

    def hidden_own():
        for r in range(2):
            for k in range(4):
                Y[tile(r, k), :] = jnp.dot(WRX[x, r], W[x * 4 + k], preferred_element_type=f32)

    def pass_on(s):
        group = (x - s + 4) % 4
        remote(
            WRX.at[group, c], WRX.at[group, c], wxsend.at[s], wxrecv.at[s], sibling
        ).wait_recv()
        go(remote(WRX.at[group, c], WRX.at[group, c], fsend.at[s], frecv.at[s], sibling))

    def hidden_add(s):
        group = (x - s + 4) % 4
        remote(
            WRX.at[group, other], WRX.at[group, other], fsend.at[s], frecv.at[s], sibling
        ).wait_recv()
        for k in range(4):
            remote(
                W.at[0], WX.at[group, k], xsend.at[0], xrecv.at[group, k], sibling
            ).wait_recv()
        for r in range(2):
            for k in range(4):
                Y[tile(r, k), :] += jnp.dot(
                    WRX[group, r], WX[group, k], preferred_element_type=f32
                )

    def hidden_end():
        for r in range(2):
            for k in range(4):
                XT[tile(r, k), :] = Y[tile(r, k), :].astype(bf16)
        for k in range(4):
            go(remote(
                XT.at[pl.ds((other * 4 + k) * 256, 256)],
                hid_out.at[:, columns(c * 1024 + k * 256, 256)],
                rsend.at[k], rrecv.at[k], sibling,
            ))
        for k in range(4):
            hid_out[:, columns(c * 1024 + k * 256, 256)] = XT[rows_at((c * 4 + k) * 256, 256), :]

    hidden_own()
    small_z()
    beside = {
        4: lambda: pass_on(1), 5: lambda: pass_on(3), 6: lambda: pass_on(2),
        8: lambda: hidden_add(1), 10: lambda: hidden_add(3), 12: lambda: hidden_add(2),
        13: hidden_end,
    }
    for step_at, (half, m) in enumerate(climb):
        sendbuf[m, row_half(half)] = total(half, m).astype(bf16)
        up(half, m)
        if step_at in beside:
            beside[step_at]()
    small_end()
    sums = small_out[...]
    small_out[...] = sums / sums[:, 2:3]
    tokens = sums[0:1, 2:3]
    for copy in m_loads:
        copy.wait()
    first = adam_direction(total(0, 0) / tokens, mom[row_half(0)], sec[row_half(0)])
    pu_out[0:CUT] = first
    second = adam_direction(total(1, 0) / tokens, mom[row_half(1)], sec[row_half(1)])
    pu_out[CUT:512] = second[:512 - CUT]
    du_out[...] = second[512 - CUT:]
    for k in range(4):
        remote(
            XT.at[pl.ds(k * 256, 256)], hid_out.at[:, columns(other * 1024 + k * 256, 256)],
            rsend.at[k], rrecv.at[k], sibling,
        ).wait_recv()

    for copy in started:
        copy.wait_send()
    for k in range(16):
        @pl.when(k // 4 != x)
        def _():
            across(k, x, k // 4).wait_send()

    def drain(i, _):
        send(near, i).wait_send()

        @pl.when(inner)
        def _():
            send(far, i).wait_send()

        return 0

    lax.fori_loop(0, CH, drain, 0)
    dx_copy.wait()


VM = pl.BlockSpec(memory_space=pltpu.VMEM)
ANY = pl.BlockSpec(memory_space=pl.ANY)
DMA = pltpu.SemaphoreType.DMA


def emit_kernel(
    dx, hid, pu, du, sums, dx_out, hid_out, pu_out, du_out, rate_out, bias_out
):
    dx_out[...] = dx[...]
    hid_out[...] = hid[...]
    pu_out[...] = pu[...]
    du_out[...] = du[...]
    turned = sums[...].T
    rate_out[...] = turned[0:1]
    bias_out[...] = turned[1:2]


def shards(
    hidden,
    inputs,
    upstream,
    proj_weight,
    delta_weight,
    decay_rate,
    step_bias,
    proj_moment,
    proj_second,
    delta_moment,
    delta_second,
    doc_lengths,
    valid_counts,
):
    def vmem(shape, dtype=f32):
        return pltpu.VMEM(shape, dtype)

    row = vmem((32, TOK))
    input_grad, hidden_grad, proj_update, delta_update, sums = pl.pallas_call(
        layer_kernel,
        out_shape=(
            jax.ShapeDtypeStruct((TOK, 2048), bf16),
            jax.ShapeDtypeStruct((TOK, 2048), bf16),
            jax.ShapeDtypeStruct((512, 256), f32),
            jax.ShapeDtypeStruct((32, 256), f32),
            jax.ShapeDtypeStruct((32, 128), f32),
        ),
        in_specs=[ANY, ANY, ANY, ANY, ANY, VM, VM, ANY, ANY, ANY, ANY, VM, VM],
        out_specs=(ANY, VM, VM, VM, VM),
        scratch_shapes=[
            vmem((16, ROWS, 256), bf16),
            vmem((2, TOK, D // 2), bf16),
            vmem((4, 4, ROWS, 256), bf16),
            vmem((2, TOK, ROWS)),
            vmem((TOK, ROWS)),
            vmem((TOK, 512), bf16),
            vmem((TOK, 32)),
            vmem((TOK, 2048), bf16),
            vmem((TOK, 2048), bf16),
            vmem((ROWS, 256)),
            vmem((ROWS, 256)),
            vmem((2048, TOK), bf16),
            vmem((2048, TOK), bf16),
            vmem((2, 2048, TOK), bf16),
            vmem((2, 2048, N), bf16),
            vmem((2, 2048, N), bf16),
            vmem((2, 2048, TOK)),
            vmem((2048, TOK)),
            vmem((TOK, 2048), bf16),
            vmem((TOK, TOK)),
            vmem((TOK, TOK)),
            vmem((TOK, TOK)),
            vmem((2, TOK, N)),
            vmem((2, TOK, N), bf16),
            row, row, row, row, row, row,
            vmem((CH, TOK, HPC)),
            vmem((CH, TOK, HPC)),
            row, row, row, row, row,
            vmem((32, 128)),
            vmem((4, 2, TOK, ROWS), bf16),
            vmem((16, ROWS, 256), bf16),
            vmem((2, 16, CUT, 256), bf16),
            vmem((32, 128)), vmem((32, 128)), vmem((4, 32, 128)), vmem((4, 32, 128)),
            DMA((2,)), DMA((4,)), DMA((4,)), DMA((4,)), DMA((2, 16)), DMA((2, 16)), DMA, DMA,
            DMA((16,)), DMA((4, 4)), DMA((2,)), DMA((4,)),
            DMA((2, CH)), DMA((2, CH)), DMA, DMA((4,)), DMA((4,)), DMA((4,)), DMA((4,)),
            DMA((2, 16)), DMA((2, 16)), DMA((4,)), DMA((4,)), DMA((7,)), DMA((7,)),
        ],
        compiler_params=pltpu.CompilerParams(
            collective_id=0, has_side_effects=True, vmem_limit_bytes=60 * 2**20
        ),
        name="layer_backward",
    )(
        hidden, inputs, upstream, proj_weight, delta_weight, decay_rate.reshape(1, 32),
        step_bias.reshape(1, 32), proj_moment, proj_second, delta_moment, delta_second,
        doc_lengths, valid_counts,
    )
    held = (input_grad, hidden_grad, proj_update, delta_update)
    line = jax.ShapeDtypeStruct((1, 32), f32)
    blocks = [pl.BlockSpec((a.shape[0] // 2, a.shape[1]), lambda i: (i, 0)) for a in held]
    input_grad, hidden_grad, proj_update, delta_update, rate_grad, bias_grad = pl.pallas_call(
        emit_kernel,
        out_shape=tuple(jax.ShapeDtypeStruct(a.shape, a.dtype) for a in held) + (line, line),
        grid=(2,),
        in_specs=blocks + [pl.BlockSpec((32, 128), lambda i: (0, 0))],
        out_specs=tuple(blocks) + (pl.BlockSpec((1, 32), lambda i: (0, 0)),) * 2,
        name="emit",
    )(*held, sums)
    return (
        input_grad[None], hidden_grad[None], rate_grad[0], bias_grad[0], proj_update, delta_update
    )


def solution(mesh):
    return jax.shard_map(
        shards,
        mesh=mesh,
        in_specs=(
            P("dp", "context", None),
            P("dp", "context", "tensor"),
            P("dp", "context", "tensor"),
            P("tensor", ("dp", "context")),
            P("tensor", ("dp", "context")),
            P("tensor"),
            P("tensor"),
            P("tensor", ("dp", "context")),
            P("tensor", ("dp", "context")),
            P("tensor", ("dp", "context")),
            P("tensor", ("dp", "context")),
            P("dp", None),
            P("dp", "context"),
        ),
        out_specs=(
            P("dp", "context", "tensor"),
            P("dp", "context", "tensor"),
            P("tensor"),
            P("tensor"),
            P("tensor", ("dp", "context")),
            P("tensor", ("dp", "context")),
        ),
        check_vma=False,
    )
```
